32 devices in a mesh: row: 4 (over y, core), col: 8 (over z, x).
Axes of the slice: x: 2, y: 2, z: 4, core: 2. Of those that a mesh axis runs over, the one named last changes fastest.
Arguments:
- density: float32 [256, 256, 128], P('row', 'col'), may hold values from 0 to 40, as said below
Outputs:
- coarse: float32 [256, 256, 128], P('row', 'col')
- moments: float32 [3, 4, 1, 1], replicated
The draws below stay inside these ranges and needn't reach their ends.
Inputs may be any that keep to these rules, and one draw needn't show every extreme that they name: Positive density.
All inputs are finite; a program needn't handle non-finite values.
Results may differ from the reference program's by a relative error of at most 0.0003.
Values sent between devices are 32-bit elements; how exact they have to be, the bound alone decides.
A program may use at most 64 MiB of HBM per device.

```python
import jax
import jax.numpy as jnp

NZ = 128
SUB = 256
NX = 256
NY = 256
NSX = 1
NSY = 1


def draw_density(key, part):
    shape = (NX, NY, NZ)
    first_key = jax.random.fold_in(key, 11)
    xs_coord = jnp.arange(NX, dtype=jnp.float32)[:, None, None]
    ys_coord = jnp.arange(NY, dtype=jnp.float32)[None, :, None]
    amp_x = 0.6 * (1.0 + 2.0 * (jnp.mod(xs_coord, SUB) + 0.5) / SUB)
    amp_y = 1.0 + 0.5 * (jnp.mod(ys_coord, SUB) + 0.5) / SUB
    noise = jax.random.truncated_normal(first_key, -4.0, 4.0, shape, jnp.float32)
    return amp_x * amp_y * jnp.exp(0.5 * noise)


def setup_inputs(seed: int = 0) -> dict:
    keys = jax.random.split(jax.random.key(seed), 2)
    density = draw_density(jax.random.fold_in(keys[1], 71), 0)
    return {"density": density}


SPLINE_TAPS = (0.0625, 0.25, 0.375, 0.25, 0.0625)
SPACINGS = (4, 8, 16)
EPSILON = 1e-6


def rolled_pass(values_in, spacing, axis_number):
    summed = SPLINE_TAPS[0] * jnp.roll(values_in, 2 * spacing, axis=axis_number)
    for tap_index in (1, 2, 3, 4):
        summed = summed + SPLINE_TAPS[tap_index] * jnp.roll(values_in, -(tap_index - 2) * spacing, axis=axis_number)
    return summed


def depth_pass(values_in, spacing):
    summed = SPLINE_TAPS[2] * values_in
    for tap_index in (0, 1, 3, 4):
        summed = summed + SPLINE_TAPS[tap_index] * jnp.roll(values_in, -(tap_index - 2) * spacing, axis=2)
    return summed


def finish_table(table, planes):
    means = table / jnp.float32(SUB * SUB * planes)
    second = means[:, 1]
    third = means[:, 2] / (second + EPSILON) ** 1.5
    fourth = means[:, 3] / (second + EPSILON) ** 2
    return jnp.stack([means[:, 0], second, third, fourth], axis=1)


def reference(density):
    current = density
    tables = []
    for spacing in SPACINGS:
        along_x = rolled_pass(current, spacing, 0)
        along_y = rolled_pass(along_x, spacing, 1)
        smoother = depth_pass(along_y, spacing)
        detail = (current - smoother).reshape(NSX, SUB, NSY, SUB, NZ)
        square = detail * detail
        tables.append(jnp.stack([
            jnp.sum(jnp.abs(detail), axis=(1, 3, 4)),
            jnp.sum(square, axis=(1, 3, 4)),
            jnp.sum(square * detail, axis=(1, 3, 4)),
            jnp.sum(square * square, axis=(1, 3, 4))]))
        current = smoother
    table = jnp.stack(tables)
    return current, finish_table(table, NZ)
```

```python
import jax
import jax.numpy as jnp
from jax import lax
from jax.experimental import pallas as pl
from jax.experimental.pallas import tpu as pltpu
from jax.sharding import PartitionSpec as P

SUB = 256


SPLINE_TAPS = (0.0625, 0.25, 0.375, 0.25, 0.0625)
SPACINGS = (4, 8, 16)
EPSILON = 1e-06


def padded_2(block, sides, width):
    for axis, dim in sides:
        count = lax.axis_size(axis)
        forward = [(i, i + 1) for i in range(count - 1)]
        forward.append((count - 1, 0))
        backward = [(target, source) for source, target in forward]
        low = lax.ppermute(
            lax.slice_in_dim(block, block.shape[dim] - width, None, axis=dim), axis, forward
        )
        high = lax.ppermute(lax.slice_in_dim(block, 0, width, axis=dim), axis, backward)
        block = jnp.concatenate([low, block, high], axis=dim)
    return block


def holed_pass(padded, spacing, axis_number, length_out):
    summed = SPLINE_TAPS[0] * lax.slice_in_dim(padded, 0, length_out, axis=axis_number)
    for tap_index in (1, 2, 3, 4):
        portion = lax.slice_in_dim(
            padded, tap_index * spacing, tap_index * spacing + length_out, axis=axis_number
        )
        summed = summed + SPLINE_TAPS[tap_index] * portion
    return summed


def depth_pass(values_in, spacing):
    summed = SPLINE_TAPS[2] * values_in
    for tap_index in (0, 1, 3, 4):
        summed = summed + SPLINE_TAPS[tap_index] * jnp.roll(
            values_in, -(tap_index - 2) * spacing, axis=2
        )
    return summed


def moment_planes(detail):
    square = detail * detail
    return jnp.stack(
        [
            jnp.sum(jnp.abs(detail), axis=2),
            jnp.sum(square, axis=2),
            jnp.sum(square * detail, axis=2),
            jnp.sum(square * square, axis=2),
        ]
    )


def finish_table(table, planes):
    means = table / jnp.float32(SUB * SUB * planes)
    second = means[:, 1]
    third = means[:, 2] / (second + EPSILON) ** 1.5
    fourth = means[:, 3] / (second + EPSILON) ** 2
    return jnp.stack([means[:, 0], second, third, fourth], axis=1)


def per_device(density):
    size_x, size_y, planes = density.shape
    plane_list = []
    current = density
    for spacing in SPACINGS:
        rows_padded = padded_2(current, (("row", 0),), 2 * spacing)
        along_x = holed_pass(rows_padded, spacing, 0, size_x)
        cols_padded = padded_2(along_x, (("col", 1),), 2 * spacing)
        along_y = holed_pass(cols_padded, spacing, 1, size_y)
        smoother = depth_pass(along_y, spacing)
        plane_list.append(moment_planes(current - smoother))
        current = smoother
    planes_all = jnp.stack(plane_list)
    count_x = lax.axis_size("row") * size_x // SUB
    count_y = lax.axis_size("col") * size_y // SUB
    rows_global = lax.axis_index("row") * size_x + jnp.arange(size_x, dtype=jnp.int32)
    cols_global = lax.axis_index("col") * size_y + jnp.arange(size_y, dtype=jnp.int32)
    onehot_x = (
        (rows_global // SUB)[:, None] == jnp.arange(count_x, dtype=jnp.int32)[None, :]
    ).astype(jnp.float32)
    onehot_y = (
        (cols_global // SUB)[:, None] == jnp.arange(count_y, dtype=jnp.int32)[None, :]
    ).astype(jnp.float32)
    partial_table = jnp.einsum(
        "xa,skxy,yb->skab", onehot_x, planes_all, onehot_y, precision=lax.Precision.HIGHEST
    )
    table = lax.psum(partial_table, ("row", "col"))
    return (current, finish_table(table, planes))


MESH = pl.DeviceIdType.MESH
ROWS, COLS = 4, 8
DEVICES = ROWS * COLS
BLOCK = (64, 32, 128)
CLASS_X, CLASS_Y, LANES = 64, 64, 128


def five_taps(low2, low1, mid, high1, high2):
    return (
        SPLINE_TAPS[0] * (low2 + high2) + SPLINE_TAPS[1] * (low1 + high1) + SPLINE_TAPS[2] * mid
    )


def class_kernel(
    x_ref, out_ref, tab_ref, send, f0, f1, back, sums, ssem, rsem, bssem, brsem, mssem, mrsem
):
    row, col = lax.axis_index("row"), lax.axis_index("col")
    me = row * COLS + col
    col_hi, col_lo = lax.div(col, 2), lax.rem(col, 2)

    def other(step):
        hi = lax.rem(col_hi + lax.rem(step + 2, 4), 4)
        lo = lax.rem(col_lo + lax.rem(lax.div(step, 4), 2), 2)
        r = lax.rem(row + lax.div(step, 8), 4)
        return r, 2 * hi + lo

    def place(ref, r, c):
        return ref.at[pl.ds(16 * r, 8), pl.ds(pl.multiple_of(8 * c, 8), 8), :]

    barrier = pltpu.get_barrier_semaphore()

    @pl.loop(1, DEVICES)
    def _(step):
        k = lax.rem(me + step, DEVICES)
        pl.semaphore_signal(
            barrier, inc=1, device_id=(lax.div(k, COLS), lax.rem(k, COLS)), device_id_type=MESH
        )

    even3 = lax.rem(lax.broadcasted_iota(jnp.int32, (8, 8, LANES), 2), 2) == 0

    def roll(v, shift, axis):
        return pltpu.roll(v, shift % v.shape[axis], axis)

    @pl.loop(0, 4)
    def _(rx):
        for ry in range(4):
            a = jnp.stack([x_ref[i, rx, pl.ds(ry, 8, stride=4), :] for i in range(8)])
            b = jnp.stack([x_ref[8 + i, rx, pl.ds(ry, 8, stride=4), :] for i in range(8)])
            send[rx * 8 + 2 * ry] = jnp.where(even3, a, roll(b, 1, 2))
            send[rx * 8 + 2 * ry + 1] = jnp.where(even3, roll(a, -1, 2), b)

    pl.semaphore_wait(barrier, DEVICES - 1)

    def forward(r, c, source_r, source_c):
        k = r * COLS + c
        return pltpu.make_async_remote_copy(
            src_ref=send.at[k],
            dst_ref=place(f0, source_r, source_c),
            send_sem=ssem.at[k],
            recv_sem=rsem.at[source_r * COLS + source_c],
            device_id=(r, c),
            device_id_type=MESH,
        )

    @pl.loop(0, DEVICES)
    def _(step):
        r, c = other(step)

        @pl.when(r * COLS + c != me)
        def _():
            forward(r, c, row, col).start()

    f0[pl.ds(16 * row, 8), pl.ds(pl.multiple_of(8 * col, 8), 8), :] = send[me]

    @pl.loop(0, DEVICES)
    def _(step):
        r, c = other(step)

        @pl.when(r * COLS + c != me)
        def _():
            forward(r, c, r, c).wait_recv()

    even2 = lax.rem(lax.broadcasted_iota(jnp.int32, (CLASS_Y, LANES), 1), 2) == 0
    lane = lax.broadcasted_iota(jnp.int32, (1, LANES), 1)

    def fill(ref):
        @pl.loop(0, 16)
        def _(it):
            for u in range(2):
                j = it * 2 + u
                r, i = lax.div(j, 8), lax.rem(j, 8)
                here = ref[16 * r + i]
                after = ref[16 * lax.rem(r + 1, 4) + i]
                ref[16 * r + 8 + i] = jnp.where(even2, roll(here, -1, 1), roll(after, 1, 1))

    def smooth_rows(src, dst, unit, r, acc):
        def body(it, acc):
            for u in range(2):
                n = 16 * r + it * 2 + u

                def at(k):
                    return src[lax.rem(n + (k * unit + CLASS_X), CLASS_X)]

                mid = src[n]
                v = five_taps(at(-2), at(-1), mid, at(1), at(2))
                v = five_taps(*(v if k == 0 else roll(v, -k * unit, 0) for k in range(-2, 3)))
                v = five_taps(*(v if k == 0 else roll(v, -4 * k * unit, 1) for k in range(-2, 3)))
                dst[n] = v
                detail = (mid - v).reshape(8, 8, LANES)
                square = detail * detail
                parts = (jnp.abs(detail), square, square * detail, square * square)
                acc = tuple(s + jnp.sum(p, axis=0) for s, p in zip(acc, parts))
            return acc

        return lax.fori_loop(0, 4, body, acc)

    def backward(r, c, source_r, source_c):
        source = source_r * COLS + source_c
        return pltpu.make_async_remote_copy(
            src_ref=place(f1, r, c),
            dst_ref=back.at[source],
            send_sem=bssem.at[r * COLS + c],
            recv_sem=brsem.at[source],
            device_id=(r, c),
            device_id_type=MESH,
        )

    total = jnp.zeros((1, LANES), jnp.float32)
    fields = (f0, f1, f0, f1)
    for scale, spacing in enumerate(SPACINGS):
        unit = spacing // 4
        src, dst = fields[scale], fields[scale + 1]
        fill(src)
        acc = (jnp.zeros((8, LANES), jnp.float32),) * 4

        def block(j, acc):
            r = lax.rem(row + j, 4)
            acc = smooth_rows(src, dst, unit, r, acc)
            if scale == len(SPACINGS) - 1:

                @pl.loop(0, COLS)
                def _(step):
                    _, c = other(step)

                    @pl.when(r * COLS + c != me)
                    def _():
                        backward(r, c, row, col).start()

            return acc

        acc = lax.fori_loop(0, 4, block, acc)
        for moment, s in enumerate(acc):
            value = jnp.sum(jnp.sum(s, axis=0, keepdims=True), axis=1, keepdims=True)
            total = total + jnp.where(lane == 4 * scale + moment, value, 0.0)

    sums[me] = total

    def share(r, c, source):
        return pltpu.make_async_remote_copy(
            src_ref=sums.at[me],
            dst_ref=sums.at[source],
            send_sem=mssem.at[r * COLS + c],
            recv_sem=mrsem.at[source],
            device_id=(r, c),
            device_id_type=MESH,
        )

    @pl.loop(0, DEVICES)
    def _(step):
        r, c = other(step)

        @pl.when(r * COLS + c != me)
        def _():
            share(r, c, me).start()

    back[me] = f1[pl.ds(16 * row, 8), pl.ds(pl.multiple_of(8 * col, 8), 8), :]

    @pl.loop(0, 4)
    def _(j):
        rx = lax.rem(row + 4 - j, 4)
        for ry in range(4):
            for p in range(2):
                k = rx * COLS + 2 * ry + p

                @pl.when(k != me)
                def _():
                    backward(rx, 2 * ry + p, rx, 2 * ry + p).wait_recv()

            p0, p1 = back[rx * COLS + 2 * ry], back[rx * COLS + 2 * ry + 1]
            a = jnp.where(even3, p0, roll(p1, 1, 2))
            b = jnp.where(even3, roll(p0, -1, 2), p1)
            for i in range(8):
                out_ref[i, rx, pl.ds(ry, 8, stride=4), :] = a[i]
                out_ref[8 + i, rx, pl.ds(ry, 8, stride=4), :] = b[i]

    @pl.loop(0, DEVICES)
    def _(step):
        r, c = other(step)
        k = r * COLS + c

        @pl.when(k != me)
        def _():
            share(r, c, k).wait_recv()
            share(r, c, k).wait_send()
            forward(r, c, r, c).wait_send()
            backward(r, c, r, c).wait_send()

    tab_ref[...] = jnp.sum(sums[...], axis=0)


def per_device_classes(density):
    size_x, size_y, planes = density.shape
    dma = pltpu.SemaphoreType.DMA((DEVICES,))
    block = pltpu.VMEM((DEVICES, 8, 8, LANES), jnp.float32)
    field = pltpu.VMEM((CLASS_X, CLASS_Y, LANES), jnp.float32)
    coarse, sums = pl.pallas_call(
        class_kernel,
        out_shape=(
            jax.ShapeDtypeStruct((16, 4, size_y, planes), jnp.float32),
            jax.ShapeDtypeStruct((1, LANES), jnp.float32),
        ),
        in_specs=[pl.BlockSpec(memory_space=pltpu.VMEM)],
        out_specs=(pl.BlockSpec(memory_space=pltpu.VMEM),) * 2,
        scratch_shapes=[
            block,
            field,
            field,
            block,
            pltpu.VMEM((DEVICES, 1, LANES), jnp.float32),
        ]
        + [dma] * 6,
        compiler_params=pltpu.CompilerParams(
            collective_id=0, has_side_effects=True, vmem_limit_bytes=32 * 1024 * 1024
        ),
    )(density.reshape(16, 4, size_y, planes))
    table = sums[0, :12].reshape(3, 4, 1, 1)
    return coarse.reshape(size_x, size_y, planes), finish_table(table, planes)


def solution(mesh):
    placed = (P("row", "col", None),)

    def program(density):
        size_x, size_y, planes = density.shape
        local = (size_x // mesh.shape["row"], size_y // mesh.shape["col"], planes)
        classes = (mesh.shape["row"], mesh.shape["col"]) == (ROWS, COLS) and local == BLOCK
        return jax.shard_map(
            per_device_classes if classes else per_device,
            mesh=mesh,
            in_specs=placed,
            out_specs=(P("row", "col", None), P()),
            check_vma=False,
        )(density)

    return program
```

```python
import jax
import jax.numpy as jnp
from jax import lax
from jax.experimental import pallas as pl
from jax.experimental.pallas import tpu as pltpu
from jax.sharding import PartitionSpec as P

SUB = 256


SPLINE_TAPS = (0.0625, 0.25, 0.375, 0.25, 0.0625)
SPACINGS = (4, 8, 16)
EPSILON = 1e-06


def padded_2(block, sides, width):
    for axis, dim in sides:
        count = lax.axis_size(axis)
        forward = [(i, i + 1) for i in range(count - 1)]
        forward.append((count - 1, 0))
        backward = [(target, source) for source, target in forward]
        low = lax.ppermute(
            lax.slice_in_dim(block, block.shape[dim] - width, None, axis=dim), axis, forward
        )
        high = lax.ppermute(lax.slice_in_dim(block, 0, width, axis=dim), axis, backward)
        block = jnp.concatenate([low, block, high], axis=dim)
    return block


def holed_pass(padded, spacing, axis_number, length_out):
    summed = SPLINE_TAPS[0] * lax.slice_in_dim(padded, 0, length_out, axis=axis_number)
    for tap_index in (1, 2, 3, 4):
        portion = lax.slice_in_dim(
            padded, tap_index * spacing, tap_index * spacing + length_out, axis=axis_number
        )
        summed = summed + SPLINE_TAPS[tap_index] * portion
    return summed


def depth_pass(values_in, spacing):
    summed = SPLINE_TAPS[2] * values_in
    for tap_index in (0, 1, 3, 4):
        summed = summed + SPLINE_TAPS[tap_index] * jnp.roll(
            values_in, -(tap_index - 2) * spacing, axis=2
        )
    return summed


def moment_planes(detail):
    square = detail * detail
    return jnp.stack(
        [
            jnp.sum(jnp.abs(detail), axis=2),
            jnp.sum(square, axis=2),
            jnp.sum(square * detail, axis=2),
            jnp.sum(square * square, axis=2),
        ]
    )


def finish_table(table, planes):
    means = table / jnp.float32(SUB * SUB * planes)
    second = means[:, 1]
    third = means[:, 2] / (second + EPSILON) ** 1.5
    fourth = means[:, 3] / (second + EPSILON) ** 2
    return jnp.stack([means[:, 0], second, third, fourth], axis=1)


def per_device(density):
    size_x, size_y, planes = density.shape
    plane_list = []
    current = density
    for spacing in SPACINGS:
        rows_padded = padded_2(current, (("row", 0),), 2 * spacing)
        along_x = holed_pass(rows_padded, spacing, 0, size_x)
        cols_padded = padded_2(along_x, (("col", 1),), 2 * spacing)
        along_y = holed_pass(cols_padded, spacing, 1, size_y)
        smoother = depth_pass(along_y, spacing)
        plane_list.append(moment_planes(current - smoother))
        current = smoother
    planes_all = jnp.stack(plane_list)
    count_x = lax.axis_size("row") * size_x // SUB
    count_y = lax.axis_size("col") * size_y // SUB
    rows_global = lax.axis_index("row") * size_x + jnp.arange(size_x, dtype=jnp.int32)
    cols_global = lax.axis_index("col") * size_y + jnp.arange(size_y, dtype=jnp.int32)
    onehot_x = (
        (rows_global // SUB)[:, None] == jnp.arange(count_x, dtype=jnp.int32)[None, :]
    ).astype(jnp.float32)
    onehot_y = (
        (cols_global // SUB)[:, None] == jnp.arange(count_y, dtype=jnp.int32)[None, :]
    ).astype(jnp.float32)
    partial_table = jnp.einsum(
        "xa,skxy,yb->skab", onehot_x, planes_all, onehot_y, precision=lax.Precision.HIGHEST
    )
    table = lax.psum(partial_table, ("row", "col"))
    return (current, finish_table(table, planes))


MESH = pl.DeviceIdType.MESH
ROWS, COLS = 4, 8
DEVICES = ROWS * COLS
BLOCK = (64, 32, 128)
CLASS_X, CLASS_Y, LANES = 64, 64, 128
CHUNKS = 2


def five_taps(low2, low1, mid, high1, high2):
    return (
        SPLINE_TAPS[0] * (low2 + high2) + SPLINE_TAPS[1] * (low1 + high1) + SPLINE_TAPS[2] * mid
    )


def roll(v, shift, axis):
    shift = shift % v.shape[axis]
    return pltpu.roll(v, shift, axis) if shift else v


def exchange_pair(lane, distance, first, second):
    clear = lax.rem(lax.div(lane, distance), 2) == 0
    return (
        jnp.where(clear, first, roll(second, distance, 2)),
        jnp.where(clear, roll(first, -distance, 2), second),
    )


def class_kernel(
    x_ref, out_ref, tab_ref, send, f0, f1, back, sums, ssem, rsem, bssem, brsem, mssem, mrsem
):
    row, col = lax.axis_index("row"), lax.axis_index("col")
    me = row * COLS + col
    col_hi, col_lo = lax.div(col, 2), lax.rem(col, 2)

    def other(step):
        hi = lax.rem(col_hi + lax.rem(step + 2, 4), 4)
        lo = lax.rem(col_lo + lax.rem(lax.div(step, 4), 2), 2)
        r = lax.rem(row + lax.div(step, 8), 4)
        return r, 2 * hi + lo

    def place(ref, h, r, c):
        return ref.at[h, pl.ds(16 * r, 4), pl.ds(pl.multiple_of(8 * c, 8), 8), :]

    barrier = pltpu.get_barrier_semaphore()

    @pl.loop(1, DEVICES)
    def _(step):
        k = lax.rem(me + step, DEVICES)
        pl.semaphore_signal(
            barrier, inc=1, device_id=(lax.div(k, COLS), lax.rem(k, COLS)), device_id_type=MESH
        )

    lane3 = lax.broadcasted_iota(jnp.int32, (4, 8, LANES), 2)

    def pack(h):
        @pl.loop(0, 4)
        def _(rx):
            for ry in range(4):
                v = [
                    jnp.stack([x_ref[4 * q + i, rx, pl.ds(ry, 8, stride=4), :] for i in range(4)])
                    for q in range(4)
                ]
                u0 = exchange_pair(lane3, 2, v[0], v[2])[h]
                u1 = exchange_pair(lane3, 2, v[1], v[3])[h]
                w0, w1 = exchange_pair(lane3, 1, u0, u1)
                send[h, rx * COLS + 2 * ry] = w0
                send[h, rx * COLS + 2 * ry + 1] = w1

    def forward(h, r, c, source_r, source_c):
        k = r * COLS + c
        return pltpu.make_async_remote_copy(
            src_ref=send.at[h, k],
            dst_ref=place(f0, h, source_r, source_c),
            send_sem=ssem.at[h, k],
            recv_sem=rsem.at[h, source_r * COLS + source_c],
            device_id=(r, c),
            device_id_type=MESH,
        )

    def send_all(h):
        @pl.loop(0, DEVICES)
        def _(step):
            r, c = other(step)

            @pl.when(r * COLS + c != me)
            def _():
                forward(h, r, c, row, col).start()

        f0[h, pl.ds(16 * row, 4), pl.ds(pl.multiple_of(8 * col, 8), 8), :] = send[h, me]

    def receive_all(h):
        @pl.loop(0, DEVICES)
        def _(step):
            r, c = other(step)

            @pl.when(r * COLS + c != me)
            def _():
                forward(h, r, c, r, c).wait_recv()

    lane2 = lax.broadcasted_iota(jnp.int32, (CLASS_Y, LANES), 1)
    lane = lax.broadcasted_iota(jnp.int32, (1, LANES), 1)

    def fill(ref, h, unit):
        @pl.loop(0, 4)
        def _(r):
            for i in range(4):
                here = ref[h, 16 * r + i]
                after = ref[h, 16 * lax.rem(r + 1, 4) + i]
                for m in (1, 2, 3):
                    reached = (i < 2 * unit, unit == 4, i >= 4 - 2 * unit)[m - 1]
                    if reached:
                        ref[h, 16 * r + 4 * m + i] = jnp.where(
                            lax.rem(lane2, 4) < 4 - m, roll(here, -m, 1), roll(after, 4 - m, 1)
                        )

    def smooth_rows(src, dst, h, unit, r, acc):
        for i in range(4):
            n = 16 * r + i

            def at(k):
                return src[h, lax.rem(n + (k * unit + CLASS_X), CLASS_X)]

            mid = src[h, n]
            v = five_taps(at(-2), at(-1), mid, at(1), at(2))
            v = five_taps(*(roll(v, -k * unit, 0) for k in range(-2, 3)))
            v = five_taps(*(roll(v, -4 * k * unit, 1) for k in range(-2, 3)))
            dst[h, n] = v
            detail = (mid - v).reshape(8, 8, LANES)
            square = detail * detail
            parts = (jnp.abs(detail), square, square * detail, square * square)
            acc = tuple(s + jnp.sum(p, axis=0) for s, p in zip(acc, parts))
        return acc

    def backward(h, r, c, source_r, source_c):
        source = source_r * COLS + source_c
        return pltpu.make_async_remote_copy(
            src_ref=place(f1, h, r, c),
            dst_ref=back.at[h, source],
            send_sem=bssem.at[h, r * COLS + c],
            recv_sem=brsem.at[h, source],
            device_id=(r, c),
            device_id_type=MESH,
        )

    def scales(h, accs):
        fields = (f0, f1, f0, f1)
        results = []
        for scale, spacing in enumerate(SPACINGS):
            unit = spacing // 4
            src, dst = fields[scale], fields[scale + 1]
            fill(src, h, unit)

            def block(j, acc):
                r = lax.rem(row + j, 4)
                acc = smooth_rows(src, dst, h, unit, r, acc)
                if scale == len(SPACINGS) - 1:

                    @pl.loop(0, COLS)
                    def _(step):
                        _, c = other(step)

                        @pl.when(r * COLS + c != me)
                        def _():
                            backward(h, r, c, row, col).start()

                return acc

            results.append(lax.fori_loop(0, 4, block, accs[scale]))
        back[h, me] = f1[h, pl.ds(16 * row, 4), pl.ds(pl.multiple_of(8 * col, 8), 8), :]
        return results

    pack(0)
    pl.semaphore_wait(barrier, DEVICES - 1)
    send_all(0)
    pack(1)
    send_all(1)
    accs = [(jnp.zeros((8, LANES), jnp.float32),) * 4] * len(SPACINGS)
    for h in range(CHUNKS):
        receive_all(h)
        accs = scales(h, accs)

    total = jnp.zeros((1, LANES), jnp.float32)
    for scale, acc in enumerate(accs):
        for moment, s in enumerate(acc):
            value = jnp.sum(jnp.sum(s, axis=0, keepdims=True), axis=1, keepdims=True)
            total = total + jnp.where(lane == 4 * scale + moment, value, 0.0)
    sums[me] = total

    def share(r, c, source):
        return pltpu.make_async_remote_copy(
            src_ref=sums.at[me],
            dst_ref=sums.at[source],
            send_sem=mssem.at[r * COLS + c],
            recv_sem=mrsem.at[source],
            device_id=(r, c),
            device_id_type=MESH,
        )

    @pl.loop(0, DEVICES)
    def _(step):
        r, c = other(step)

        @pl.when(r * COLS + c != me)
        def _():
            share(r, c, me).start()

    @pl.loop(0, 4)
    def _(j):
        rx = lax.rem(row + 4 - j, 4)
        for ry in range(4):
            u = []
            for h in range(CHUNKS):
                for p in range(2):
                    c = 2 * ry + p

                    @pl.when(rx * COLS + c != me)
                    def _():
                        backward(h, rx, c, rx, c).wait_recv()

                u.append(
                    exchange_pair(
                        lane3, 1, back[h, rx * COLS + 2 * ry], back[h, rx * COLS + 2 * ry + 1]
                    )
                )
            for q in range(2):
                for low, v in enumerate(exchange_pair(lane3, 2, u[0][q], u[1][q])):
                    for i in range(4):
                        out_ref[4 * (q + 2 * low) + i, rx, pl.ds(ry, 8, stride=4), :] = v[i]

    @pl.loop(0, DEVICES)
    def _(step):
        r, c = other(step)
        k = r * COLS + c

        @pl.when(k != me)
        def _():
            share(r, c, k).wait_recv()
            share(r, c, k).wait_send()
            for h in range(CHUNKS):
                forward(h, r, c, r, c).wait_send()
                backward(h, r, c, r, c).wait_send()

    tab_ref[...] = jnp.sum(sums[...], axis=0)


def per_device_classes(density):
    size_x, size_y, planes = density.shape
    dma = pltpu.SemaphoreType.DMA((CHUNKS, DEVICES))
    one = pltpu.SemaphoreType.DMA((DEVICES,))
    block = pltpu.VMEM((CHUNKS, DEVICES, 4, 8, LANES), jnp.float32)
    field = pltpu.VMEM((CHUNKS, CLASS_X, CLASS_Y, LANES), jnp.float32)
    coarse, sums = pl.pallas_call(
        class_kernel,
        out_shape=(
            jax.ShapeDtypeStruct((16, 4, size_y, planes), jnp.float32),
            jax.ShapeDtypeStruct((1, LANES), jnp.float32),
        ),
        in_specs=[pl.BlockSpec(memory_space=pltpu.VMEM)],
        out_specs=(pl.BlockSpec(memory_space=pltpu.VMEM),) * 2,
        scratch_shapes=[
            block,
            field,
            field,
            block,
            pltpu.VMEM((DEVICES, 1, LANES), jnp.float32),
        ]
        + [dma] * 4
        + [one] * 2,
        compiler_params=pltpu.CompilerParams(
            collective_id=0, has_side_effects=True, vmem_limit_bytes=32 * 1024 * 1024
        ),
    )(density.reshape(16, 4, size_y, planes))
    table = sums[0, :12].reshape(3, 4, 1, 1)
    return coarse.reshape(size_x, size_y, planes), finish_table(table, planes)


def solution(mesh):
    placed = (P("row", "col", None),)

    def program(density):
        size_x, size_y, planes = density.shape
        local = (size_x // mesh.shape["row"], size_y // mesh.shape["col"], planes)
        classes = (mesh.shape["row"], mesh.shape["col"]) == (ROWS, COLS) and local == BLOCK
        return jax.shard_map(
            per_device_classes if classes else per_device,
            mesh=mesh,
            in_specs=placed,
            out_specs=(P("row", "col", None), P()),
            check_vma=False,
        )(density)

    return program
```

```python
import jax
import jax.numpy as jnp
from jax import lax
from jax.experimental import pallas as pl
from jax.experimental.pallas import tpu as pltpu
from jax.sharding import PartitionSpec as P

SUB = 256


SPLINE_TAPS = (0.0625, 0.25, 0.375, 0.25, 0.0625)
SPACINGS = (4, 8, 16)
EPSILON = 1e-06


def padded_2(block, sides, width):
    for axis, dim in sides:
        count = lax.axis_size(axis)
        forward = [(i, i + 1) for i in range(count - 1)]
        forward.append((count - 1, 0))
        backward = [(target, source) for source, target in forward]
        low = lax.ppermute(
            lax.slice_in_dim(block, block.shape[dim] - width, None, axis=dim), axis, forward
        )
        high = lax.ppermute(lax.slice_in_dim(block, 0, width, axis=dim), axis, backward)
        block = jnp.concatenate([low, block, high], axis=dim)
    return block


def holed_pass(padded, spacing, axis_number, length_out):
    summed = SPLINE_TAPS[0] * lax.slice_in_dim(padded, 0, length_out, axis=axis_number)
    for tap_index in (1, 2, 3, 4):
        portion = lax.slice_in_dim(
            padded, tap_index * spacing, tap_index * spacing + length_out, axis=axis_number
        )
        summed = summed + SPLINE_TAPS[tap_index] * portion
    return summed


def depth_pass(values_in, spacing):
    summed = SPLINE_TAPS[2] * values_in
    for tap_index in (0, 1, 3, 4):
        summed = summed + SPLINE_TAPS[tap_index] * jnp.roll(
            values_in, -(tap_index - 2) * spacing, axis=2
        )
    return summed


def moment_planes(detail):
    square = detail * detail
    return jnp.stack(
        [
            jnp.sum(jnp.abs(detail), axis=2),
            jnp.sum(square, axis=2),
            jnp.sum(square * detail, axis=2),
            jnp.sum(square * square, axis=2),
        ]
    )


def finish_table(table, planes):
    means = table / jnp.float32(SUB * SUB * planes)
    second = means[:, 1]
    third = means[:, 2] / (second + EPSILON) ** 1.5
    fourth = means[:, 3] / (second + EPSILON) ** 2
    return jnp.stack([means[:, 0], second, third, fourth], axis=1)


def per_device(density):
    size_x, size_y, planes = density.shape
    plane_list = []
    current = density
    for spacing in SPACINGS:
        rows_padded = padded_2(current, (("row", 0),), 2 * spacing)
        along_x = holed_pass(rows_padded, spacing, 0, size_x)
        cols_padded = padded_2(along_x, (("col", 1),), 2 * spacing)
        along_y = holed_pass(cols_padded, spacing, 1, size_y)
        smoother = depth_pass(along_y, spacing)
        plane_list.append(moment_planes(current - smoother))
        current = smoother
    planes_all = jnp.stack(plane_list)
    count_x = lax.axis_size("row") * size_x // SUB
    count_y = lax.axis_size("col") * size_y // SUB
    rows_global = lax.axis_index("row") * size_x + jnp.arange(size_x, dtype=jnp.int32)
    cols_global = lax.axis_index("col") * size_y + jnp.arange(size_y, dtype=jnp.int32)
    onehot_x = (
        (rows_global // SUB)[:, None] == jnp.arange(count_x, dtype=jnp.int32)[None, :]
    ).astype(jnp.float32)
    onehot_y = (
        (cols_global // SUB)[:, None] == jnp.arange(count_y, dtype=jnp.int32)[None, :]
    ).astype(jnp.float32)
    partial_table = jnp.einsum(
        "xa,skxy,yb->skab", onehot_x, planes_all, onehot_y, precision=lax.Precision.HIGHEST
    )
    table = lax.psum(partial_table, ("row", "col"))
    return (current, finish_table(table, planes))


MESH = pl.DeviceIdType.MESH
ROWS, COLS = 4, 8
DEVICES = ROWS * COLS
BLOCK = (64, 32, 128)
CLASS_X, CLASS_Y, LANES = 64, 64, 128
CHUNKS = 2


def five_taps(low2, low1, mid, high1, high2):
    return (
        SPLINE_TAPS[0] * (low2 + high2) + SPLINE_TAPS[1] * (low1 + high1) + SPLINE_TAPS[2] * mid
    )


def roll(v, shift, axis):
    shift = shift % v.shape[axis]
    return pltpu.roll(v, shift, axis) if shift else v


def exchange_pair(lane, distance, first, second):
    clear = lax.rem(lax.div(lane, distance), 2) == 0
    return (
        jnp.where(clear, first, roll(second, distance, 2)),
        jnp.where(clear, roll(first, -distance, 2), second),
    )


def class_kernel(
    x_hbm,
    out_ref,
    tab_ref,
    x_ref,
    send,
    f0,
    f1,
    back,
    padded,
    taps,
    sums,
    ssem,
    rsem,
    bssem,
    brsem,
    mssem,
    mrsem,
    xsem,
):
    row, col = lax.axis_index("row"), lax.axis_index("col")
    me = row * COLS + col
    col_hi, col_lo = lax.div(col, 2), lax.rem(col, 2)

    def other(step):
        hi = lax.rem(col_hi + lax.rem(step + 2, 4), 4)
        lo = lax.rem(col_lo + lax.rem(lax.div(step, 4), 2), 2)
        r = lax.rem(row + lax.div(step, 8), 4)
        return r, 2 * hi + lo

    def place(ref, h, r, c):
        return ref.at[h, 4 * r, c]

    def load_x(rx):
        return pltpu.make_async_copy(x_hbm.at[:, rx], x_ref.at[:, rx], xsem.at[rx])

    for rx in range(4):
        load_x(rx).start()

    barrier = pltpu.get_barrier_semaphore()

    @pl.loop(1, DEVICES)
    def _(step):
        k = lax.rem(me + step, DEVICES)
        pl.semaphore_signal(
            barrier, inc=1, device_id=(lax.div(k, COLS), lax.rem(k, COLS)), device_id_type=MESH
        )

    lane3 = lax.broadcasted_iota(jnp.int32, (4, 8, LANES), 2)

    def pack(h):
        @pl.loop(0, 4)
        def _(rx):
            if h == 0:
                load_x(rx).wait()
            for ry in range(4):
                v = [
                    jnp.stack([x_ref[4 * q + i, rx, pl.ds(ry, 8, stride=4), :] for i in range(4)])
                    for q in range(4)
                ]
                u0 = exchange_pair(lane3, 2, v[0], v[2])[h]
                u1 = exchange_pair(lane3, 2, v[1], v[3])[h]
                w0, w1 = exchange_pair(lane3, 1, u0, u1)
                send[h, rx * COLS + 2 * ry] = w0
                send[h, rx * COLS + 2 * ry + 1] = w1

    def forward(h, r, c, source_r, source_c):
        k = r * COLS + c
        return pltpu.make_async_remote_copy(
            src_ref=send.at[h, k],
            dst_ref=place(f0, h, source_r, source_c),
            send_sem=ssem.at[h, k],
            recv_sem=rsem.at[h, source_r * COLS + source_c],
            device_id=(r, c),
            device_id_type=MESH,
        )

    def send_all(h):
        @pl.loop(0, DEVICES)
        def _(step):
            r, c = other(step)

            @pl.when(r * COLS + c != me)
            def _():
                forward(h, r, c, row, col).start()

        f0[h, 4 * row, col] = send[h, me]

    def receive_all(h):
        @pl.loop(0, DEVICES)
        def _(step):
            r, c = other(step)

            @pl.when(r * COLS + c != me)
            def _():
                forward(h, r, c, r, c).wait_recv()

    lane2 = lax.broadcasted_iota(jnp.int32, (CLASS_Y, LANES), 1)
    lane = lax.broadcasted_iota(jnp.int32, (1, LANES), 1)

    def fill(ref, h, unit):
        @pl.loop(0, 4)
        def _(r):
            for i in range(4):
                here = ref[h, 4 * r, :, i].reshape(CLASS_Y, LANES)
                after = ref[h, 4 * lax.rem(r + 1, 4), :, i].reshape(CLASS_Y, LANES)
                for m in (1, 2, 3):
                    reached = (i < 2 * unit, unit == 4, i >= 4 - 2 * unit)[m - 1]
                    if reached:
                        ref[h, 4 * r + m, :, i] = jnp.where(
                            lax.rem(lane2, 4) < 4 - m, roll(here, -m, 1), roll(after, 4 - m, 1)
                        ).reshape(8, 8, LANES)

    def make_taps():
        shape = (2 * LANES, LANES)
        gap = lax.rem(
            lax.broadcasted_iota(jnp.int32, shape, 0)
            - lax.broadcasted_iota(jnp.int32, shape, 1)
            + LANES,
            LANES,
        )
        for scale, spacing in enumerate(SPACINGS):
            matrix = jnp.zeros(shape, jnp.float32)
            for k, tap in zip(range(-2, 3), SPLINE_TAPS):
                matrix = jnp.where(gap == (k * spacing) % LANES, tap, matrix)
            taps[scale] = matrix.astype(jnp.bfloat16)

    def smooth_rows(src, dst, h, scale, r, acc):
        unit = SPACINGS[scale] // 4
        mids = []
        for i in range(4):

            def at(k):
                n = i + k * unit
                return src[h, lax.rem(4 * r + (n // 4 + 16), 16), :, n % 4].reshape(CLASS_Y, LANES)

            mids.append(at(0))
            v = five_taps(at(-2), at(-1), mids[i], at(1), at(2))
            padded[i, 8:72, :] = v
            padded[i, 0:8, :] = v[56:]
            padded[i, 72:80, :] = v[:8]
        rows = []
        for i in range(4):
            rows.append(
                five_taps(*(padded[i, 8 + k * unit : 72 + k * unit, :] for k in range(-2, 3)))
            )
        v = jnp.concatenate(rows, axis=0)
        high = v.astype(jnp.bfloat16)
        low = (v - high.astype(jnp.float32)).astype(jnp.bfloat16)
        v = jnp.dot(
            jnp.concatenate([high, low], axis=1), taps[scale], preferred_element_type=jnp.float32
        )
        for i in range(4):
            smooth = v[CLASS_Y * i : CLASS_Y * (i + 1)]
            dst[h, 4 * r, :, i] = smooth.reshape(8, 8, LANES)
            detail = (mids[i] - smooth).reshape(8, 8, LANES)
            square = detail * detail
            parts = (jnp.abs(detail), square, square * detail, square * square)
            acc = tuple(s + jnp.sum(p, axis=0) for s, p in zip(acc, parts))
        return acc

    def backward(h, r, c, source_r, source_c):
        source = source_r * COLS + source_c
        return pltpu.make_async_remote_copy(
            src_ref=place(f1, h, r, c),
            dst_ref=back.at[h, source],
            send_sem=bssem.at[h, r * COLS + c],
            recv_sem=brsem.at[h, source],
            device_id=(r, c),
            device_id_type=MESH,
        )

    def scales(h, accs):
        fields = (f0, f1, f0, f1)
        results = []
        for scale, spacing in enumerate(SPACINGS):
            src, dst = fields[scale], fields[scale + 1]
            fill(src, h, spacing // 4)

            def block(j, acc):
                r = lax.rem(row + j, 4)
                acc = smooth_rows(src, dst, h, scale, r, acc)
                if scale == len(SPACINGS) - 1:

                    @pl.loop(0, COLS)
                    def _(step):
                        _, c = other(step)

                        @pl.when(r * COLS + c != me)
                        def _():
                            backward(h, r, c, row, col).start()

                return acc

            results.append(lax.fori_loop(0, 4, block, accs[scale]))
        back[h, me] = f1[h, 4 * row, col]
        return results

    make_taps()
    pack(0)
    pl.semaphore_wait(barrier, DEVICES - 1)
    send_all(0)
    pack(1)
    send_all(1)
    accs = [(jnp.zeros((8, LANES), jnp.float32),) * 4] * len(SPACINGS)
    for h in range(CHUNKS):
        receive_all(h)
        accs = scales(h, accs)

    total = jnp.zeros((1, LANES), jnp.float32)
    for scale, acc in enumerate(accs):
        for moment, s in enumerate(acc):
            value = jnp.sum(jnp.sum(s, axis=0, keepdims=True), axis=1, keepdims=True)
            total = total + jnp.where(lane == 4 * scale + moment, value, 0.0)
    sums[me] = total

    def share(r, c, source):
        return pltpu.make_async_remote_copy(
            src_ref=sums.at[me],
            dst_ref=sums.at[source],
            send_sem=mssem.at[r * COLS + c],
            recv_sem=mrsem.at[source],
            device_id=(r, c),
            device_id_type=MESH,
        )

    @pl.loop(0, DEVICES)
    def _(step):
        r, c = other(step)

        @pl.when(r * COLS + c != me)
        def _():
            share(r, c, me).start()

    @pl.loop(0, 4)
    def _(j):
        rx = lax.rem(row + 4 - j, 4)
        for ry in range(4):
            u = []
            for h in range(CHUNKS):
                for p in range(2):
                    c = 2 * ry + p

                    @pl.when(rx * COLS + c != me)
                    def _():
                        backward(h, rx, c, rx, c).wait_recv()

                u.append(
                    exchange_pair(
                        lane3, 1, back[h, rx * COLS + 2 * ry], back[h, rx * COLS + 2 * ry + 1]
                    )
                )
            for q in range(2):
                for low, v in enumerate(exchange_pair(lane3, 2, u[0][q], u[1][q])):
                    for i in range(4):
                        out_ref[4 * (q + 2 * low) + i, rx, pl.ds(ry, 8, stride=4), :] = v[i]

    @pl.loop(0, DEVICES)
    def _(step):
        r, c = other(step)
        k = r * COLS + c

        @pl.when(k != me)
        def _():
            share(r, c, k).wait_recv()
            share(r, c, k).wait_send()
            for h in range(CHUNKS):
                forward(h, r, c, r, c).wait_send()
                backward(h, r, c, r, c).wait_send()

    tab_ref[...] = jnp.sum(sums[...], axis=0)


def per_device_classes(density):
    size_x, size_y, planes = density.shape
    dma = pltpu.SemaphoreType.DMA((CHUNKS, DEVICES))
    one = pltpu.SemaphoreType.DMA((DEVICES,))
    block = pltpu.VMEM((CHUNKS, DEVICES, 4, 8, LANES), jnp.float32)
    field = pltpu.VMEM((CHUNKS, CLASS_X // 4, CLASS_Y // 8, 4, 8, LANES), jnp.float32)
    coarse, sums = pl.pallas_call(
        class_kernel,
        out_shape=(
            jax.ShapeDtypeStruct((16, 4, size_y, planes), jnp.float32),
            jax.ShapeDtypeStruct((1, LANES), jnp.float32),
        ),
        in_specs=[pl.BlockSpec(memory_space=pltpu.HBM)],
        out_specs=(pl.BlockSpec(memory_space=pltpu.VMEM),) * 2,
        scratch_shapes=[
            pltpu.VMEM((16, 4, size_y, planes), jnp.float32),
            block,
            field,
            field,
            block,
            pltpu.VMEM((4, CLASS_Y + 16, LANES), jnp.float32),
            pltpu.VMEM((len(SPACINGS), 2 * LANES, LANES), jnp.bfloat16),
            pltpu.VMEM((DEVICES, 1, LANES), jnp.float32),
        ]
        + [dma] * 4
        + [one] * 2
        + [pltpu.SemaphoreType.DMA((4,))],
        compiler_params=pltpu.CompilerParams(
            collective_id=0, has_side_effects=True, vmem_limit_bytes=32 * 1024 * 1024
        ),
    )(density.reshape(16, 4, size_y, planes))
    table = sums[0, :12].reshape(3, 4, 1, 1)
    return coarse.reshape(size_x, size_y, planes), finish_table(table, planes)


def solution(mesh):
    placed = (P("row", "col", None),)

    def program(density):
        size_x, size_y, planes = density.shape
        local = (size_x // mesh.shape["row"], size_y // mesh.shape["col"], planes)
        classes = (mesh.shape["row"], mesh.shape["col"]) == (ROWS, COLS) and local == BLOCK
        return jax.shard_map(
            per_device_classes if classes else per_device,
            mesh=mesh,
            in_specs=placed,
            out_specs=(P("row", "col", None), P()),
            check_vma=False,
        )(density)

    return program
```

```python
import jax
import jax.numpy as jnp
from jax import lax
from jax.experimental import pallas as pl
from jax.experimental.pallas import tpu as pltpu
from jax.sharding import PartitionSpec as P

SUB = 256


SPLINE_TAPS = (0.0625, 0.25, 0.375, 0.25, 0.0625)
SPACINGS = (4, 8, 16)
EPSILON = 1e-06


def padded_2(block, sides, width):
    for axis, dim in sides:
        count = lax.axis_size(axis)
        forward = [(i, i + 1) for i in range(count - 1)]
        forward.append((count - 1, 0))
        backward = [(target, source) for source, target in forward]
        low = lax.ppermute(
            lax.slice_in_dim(block, block.shape[dim] - width, None, axis=dim), axis, forward
        )
        high = lax.ppermute(lax.slice_in_dim(block, 0, width, axis=dim), axis, backward)
        block = jnp.concatenate([low, block, high], axis=dim)
    return block


def holed_pass(padded, spacing, axis_number, length_out):
    summed = SPLINE_TAPS[0] * lax.slice_in_dim(padded, 0, length_out, axis=axis_number)
    for tap_index in (1, 2, 3, 4):
        portion = lax.slice_in_dim(
            padded, tap_index * spacing, tap_index * spacing + length_out, axis=axis_number
        )
        summed = summed + SPLINE_TAPS[tap_index] * portion
    return summed


def depth_pass(values_in, spacing):
    summed = SPLINE_TAPS[2] * values_in
    for tap_index in (0, 1, 3, 4):
        summed = summed + SPLINE_TAPS[tap_index] * jnp.roll(
            values_in, -(tap_index - 2) * spacing, axis=2
        )
    return summed


def moment_planes(detail):
    square = detail * detail
    return jnp.stack(
        [
            jnp.sum(jnp.abs(detail), axis=2),
            jnp.sum(square, axis=2),
            jnp.sum(square * detail, axis=2),
            jnp.sum(square * square, axis=2),
        ]
    )


def finish_table(table, planes):
    means = table / jnp.float32(SUB * SUB * planes)
    second = means[:, 1]
    third = means[:, 2] / (second + EPSILON) ** 1.5
    fourth = means[:, 3] / (second + EPSILON) ** 2
    return jnp.stack([means[:, 0], second, third, fourth], axis=1)


def per_device(density):
    size_x, size_y, planes = density.shape
    plane_list = []
    current = density
    for spacing in SPACINGS:
        rows_padded = padded_2(current, (("row", 0),), 2 * spacing)
        along_x = holed_pass(rows_padded, spacing, 0, size_x)
        cols_padded = padded_2(along_x, (("col", 1),), 2 * spacing)
        along_y = holed_pass(cols_padded, spacing, 1, size_y)
        smoother = depth_pass(along_y, spacing)
        plane_list.append(moment_planes(current - smoother))
        current = smoother
    planes_all = jnp.stack(plane_list)
    count_x = lax.axis_size("row") * size_x // SUB
    count_y = lax.axis_size("col") * size_y // SUB
    rows_global = lax.axis_index("row") * size_x + jnp.arange(size_x, dtype=jnp.int32)
    cols_global = lax.axis_index("col") * size_y + jnp.arange(size_y, dtype=jnp.int32)
    onehot_x = (
        (rows_global // SUB)[:, None] == jnp.arange(count_x, dtype=jnp.int32)[None, :]
    ).astype(jnp.float32)
    onehot_y = (
        (cols_global // SUB)[:, None] == jnp.arange(count_y, dtype=jnp.int32)[None, :]
    ).astype(jnp.float32)
    partial_table = jnp.einsum(
        "xa,skxy,yb->skab", onehot_x, planes_all, onehot_y, precision=lax.Precision.HIGHEST
    )
    table = lax.psum(partial_table, ("row", "col"))
    return (current, finish_table(table, planes))


MESH = pl.DeviceIdType.MESH
ROWS, COLS = 4, 8
DEVICES = ROWS * COLS
BLOCK = (64, 32, 128)
CLASS_X, CLASS_Y, LANES = 64, 64, 128
CHUNKS = 2


def five_taps(low2, low1, mid, high1, high2):
    return (
        SPLINE_TAPS[0] * (low2 + high2) + SPLINE_TAPS[1] * (low1 + high1) + SPLINE_TAPS[2] * mid
    )


def roll(v, shift, axis):
    shift = shift % v.shape[axis]
    return pltpu.roll(v, shift, axis) if shift else v


def exchange_pair(lane, distance, first, second):
    clear = lax.rem(lax.div(lane, distance), 2) == 0
    return (
        jnp.where(clear, first, roll(second, distance, 2)),
        jnp.where(clear, roll(first, -distance, 2), second),
    )


def class_kernel(
    x_hbm,
    out_ref,
    tab_ref,
    x_ref,
    send,
    f0,
    f1,
    back,
    padded,
    taps,
    sums,
    ssem,
    rsem,
    bssem,
    brsem,
    mssem,
    mrsem,
    xsem,
):
    row, col = lax.axis_index("row"), lax.axis_index("col")
    me = row * COLS + col
    col_hi, col_lo = lax.div(col, 2), lax.rem(col, 2)

    order = jnp.where(
        col_hi == 0, 30, jnp.where(col_hi == 1, 180, jnp.where(col_hi == 2, 75, 225))
    )

    def each_other(visit):
        for step in range(4):
            hi = lax.rem(lax.div(order, 4**step), 4)

            @pl.loop(0, DEVICES // 4)
            def _(near):
                c = 2 * hi + lax.rem(col_lo + lax.rem(near, 2), 2)
                r = lax.rem(row + lax.div(near, 2), 4)

                @pl.when(r * COLS + c != me)
                def _():
                    visit(r, c)

    def place(ref, h, r, c):
        return ref.at[h, 4 * r, c]

    def load_x(rx):
        return pltpu.make_async_copy(x_hbm.at[:, rx], x_ref.at[:, rx], xsem.at[rx])

    for rx in range(4):
        load_x(rx).start()

    barrier = pltpu.get_barrier_semaphore()

    @pl.loop(1, DEVICES)
    def _(step):
        k = lax.rem(me + step, DEVICES)
        pl.semaphore_signal(
            barrier, inc=1, device_id=(lax.div(k, COLS), lax.rem(k, COLS)), device_id_type=MESH
        )

    lane3 = lax.broadcasted_iota(jnp.int32, (4, 8, LANES), 2)

    def pack(h):
        @pl.loop(0, 4)
        def _(rx):
            if h == 0:
                load_x(rx).wait()
            for ry in range(4):
                v = [
                    jnp.stack([x_ref[4 * q + i, rx, pl.ds(ry, 8, stride=4), :] for i in range(4)])
                    for q in range(4)
                ]
                u0 = exchange_pair(lane3, 2, v[0], v[2])[h]
                u1 = exchange_pair(lane3, 2, v[1], v[3])[h]
                w0, w1 = exchange_pair(lane3, 1, u0, u1)
                send[h, rx * COLS + 2 * ry] = w0
                send[h, rx * COLS + 2 * ry + 1] = w1

    def forward(h, r, c, source_r, source_c):
        k = r * COLS + c
        return pltpu.make_async_remote_copy(
            src_ref=send.at[h, k],
            dst_ref=place(f0, h, source_r, source_c),
            send_sem=ssem.at[h, k],
            recv_sem=rsem.at[h, source_r * COLS + source_c],
            device_id=(r, c),
            device_id_type=MESH,
        )

    def send_all(h):
        each_other(lambda r, c: forward(h, r, c, row, col).start())
        f0[h, 4 * row, col] = send[h, me]

    def receive_all(h):
        each_other(lambda r, c: forward(h, r, c, r, c).wait_recv())

    lane2 = lax.broadcasted_iota(jnp.int32, (CLASS_Y, LANES), 1)
    lane = lax.broadcasted_iota(jnp.int32, (1, LANES), 1)

    def fill(ref, h, unit):
        @pl.loop(0, 4)
        def _(r):
            for i in range(4):
                here = ref[h, 4 * r, :, i].reshape(CLASS_Y, LANES)
                after = ref[h, 4 * lax.rem(r + 1, 4), :, i].reshape(CLASS_Y, LANES)
                for m in (1, 2, 3):
                    reached = (i < 2 * unit, unit == 4, i >= 4 - 2 * unit)[m - 1]
                    if reached:
                        ref[h, 4 * r + m, :, i] = jnp.where(
                            lax.rem(lane2, 4) < 4 - m, roll(here, -m, 1), roll(after, 4 - m, 1)
                        ).reshape(8, 8, LANES)

    def make_taps():
        shape = (2 * LANES, LANES)
        gap = lax.rem(
            lax.broadcasted_iota(jnp.int32, shape, 0)
            - lax.broadcasted_iota(jnp.int32, shape, 1)
            + LANES,
            LANES,
        )
        for scale, spacing in enumerate(SPACINGS):
            matrix = jnp.zeros(shape, jnp.float32)
            for k, tap in zip(range(-2, 3), SPLINE_TAPS):
                matrix = jnp.where(gap == (k * spacing) % LANES, tap, matrix)
            taps[scale] = matrix.astype(jnp.bfloat16)

    def smooth_rows(src, dst, h, scale, r, acc):
        unit = SPACINGS[scale] // 4
        mids = []
        for i in range(4):

            def at(k):
                n = i + k * unit
                return src[h, lax.rem(4 * r + (n // 4 + 16), 16), :, n % 4].reshape(CLASS_Y, LANES)

            mids.append(at(0))
            v = five_taps(at(-2), at(-1), mids[i], at(1), at(2))
            padded[i, 8:72, :] = v
            padded[i, 0:8, :] = v[56:]
            padded[i, 72:80, :] = v[:8]
        rows = []
        for i in range(4):
            rows.append(
                five_taps(*(padded[i, 8 + k * unit : 72 + k * unit, :] for k in range(-2, 3)))
            )
        v = jnp.concatenate(rows, axis=0)
        high = v.astype(jnp.bfloat16)
        low = (v - high.astype(jnp.float32)).astype(jnp.bfloat16)
        v = jnp.dot(
            jnp.concatenate([high, low], axis=1), taps[scale], preferred_element_type=jnp.float32
        )
        for i in range(4):
            smooth = v[CLASS_Y * i : CLASS_Y * (i + 1)]
            dst[h, 4 * r, :, i] = smooth.reshape(8, 8, LANES)
            detail = (mids[i] - smooth).reshape(8, 8, LANES)
            square = detail * detail
            parts = (jnp.abs(detail), square, square * detail, square * square)
            acc = tuple(s + jnp.sum(p, axis=0) for s, p in zip(acc, parts))
        return acc

    def backward(h, r, c, source_r, source_c):
        source = source_r * COLS + source_c
        return pltpu.make_async_remote_copy(
            src_ref=place(f1, h, r, c),
            dst_ref=back.at[h, source],
            send_sem=bssem.at[h, r * COLS + c],
            recv_sem=brsem.at[h, source],
            device_id=(r, c),
            device_id_type=MESH,
        )

    def scales(h, accs):
        fields = (f0, f1, f0, f1)
        results = []
        for scale, spacing in enumerate(SPACINGS):
            src, dst = fields[scale], fields[scale + 1]
            fill(src, h, spacing // 4)

            def block(j, acc):
                r = lax.rem(row + j, 4)
                return smooth_rows(src, dst, h, scale, r, acc)

            results.append(lax.fori_loop(0, 4, block, accs[scale]))
        each_other(lambda r, c: backward(h, r, c, row, col).start())
        back[h, me] = f1[h, 4 * row, col]
        return results

    make_taps()
    pack(0)
    pl.semaphore_wait(barrier, DEVICES - 1)
    send_all(0)
    pack(1)
    send_all(1)
    accs = [(jnp.zeros((8, LANES), jnp.float32),) * 4] * len(SPACINGS)
    for h in range(CHUNKS):
        receive_all(h)
        accs = scales(h, accs)

    total = jnp.zeros((1, LANES), jnp.float32)
    for scale, acc in enumerate(accs):
        for moment, s in enumerate(acc):
            value = jnp.sum(jnp.sum(s, axis=0, keepdims=True), axis=1, keepdims=True)
            total = total + jnp.where(lane == 4 * scale + moment, value, 0.0)
    sums[me] = total

    def share(r, c, source):
        return pltpu.make_async_remote_copy(
            src_ref=sums.at[me],
            dst_ref=sums.at[source],
            send_sem=mssem.at[r * COLS + c],
            recv_sem=mrsem.at[source],
            device_id=(r, c),
            device_id_type=MESH,
        )

    each_other(lambda r, c: share(r, c, me).start())

    @pl.loop(0, 4)
    def _(j):
        rx = lax.rem(row + 4 - j, 4)
        for ry in range(4):
            u = []
            for h in range(CHUNKS):
                for p in range(2):
                    c = 2 * ry + p

                    @pl.when(rx * COLS + c != me)
                    def _():
                        backward(h, rx, c, rx, c).wait_recv()

                u.append(
                    exchange_pair(
                        lane3, 1, back[h, rx * COLS + 2 * ry], back[h, rx * COLS + 2 * ry + 1]
                    )
                )
            for q in range(2):
                for low, v in enumerate(exchange_pair(lane3, 2, u[0][q], u[1][q])):
                    for i in range(4):
                        out_ref[4 * (q + 2 * low) + i, rx, pl.ds(ry, 8, stride=4), :] = v[i]

    def finish(r, c):
        share(r, c, r * COLS + c).wait_recv()
        share(r, c, r * COLS + c).wait_send()
        for h in range(CHUNKS):
            forward(h, r, c, r, c).wait_send()
            backward(h, r, c, r, c).wait_send()

    each_other(finish)

    tab_ref[...] = jnp.sum(sums[...], axis=0)


def per_device_classes(density):
    size_x, size_y, planes = density.shape
    dma = pltpu.SemaphoreType.DMA((CHUNKS, DEVICES))
    one = pltpu.SemaphoreType.DMA((DEVICES,))
    block = pltpu.VMEM((CHUNKS, DEVICES, 4, 8, LANES), jnp.float32)
    field = pltpu.VMEM((CHUNKS, CLASS_X // 4, CLASS_Y // 8, 4, 8, LANES), jnp.float32)
    coarse, sums = pl.pallas_call(
        class_kernel,
        out_shape=(
            jax.ShapeDtypeStruct((16, 4, size_y, planes), jnp.float32),
            jax.ShapeDtypeStruct((1, LANES), jnp.float32),
        ),
        in_specs=[pl.BlockSpec(memory_space=pltpu.HBM)],
        out_specs=(pl.BlockSpec(memory_space=pltpu.VMEM),) * 2,
        scratch_shapes=[
            pltpu.VMEM((16, 4, size_y, planes), jnp.float32),
            block,
            field,
            field,
            block,
            pltpu.VMEM((4, CLASS_Y + 16, LANES), jnp.float32),
            pltpu.VMEM((len(SPACINGS), 2 * LANES, LANES), jnp.bfloat16),
            pltpu.VMEM((DEVICES, 1, LANES), jnp.float32),
        ]
        + [dma] * 4
        + [one] * 2
        + [pltpu.SemaphoreType.DMA((4,))],
        compiler_params=pltpu.CompilerParams(
            collective_id=0, has_side_effects=True, vmem_limit_bytes=32 * 1024 * 1024
        ),
    )(density.reshape(16, 4, size_y, planes))
    table = sums[0, :12].reshape(3, 4, 1, 1)
    return coarse.reshape(size_x, size_y, planes), finish_table(table, planes)


def solution(mesh):
    placed = (P("row", "col", None),)

    def program(density):
        size_x, size_y, planes = density.shape
        local = (size_x // mesh.shape["row"], size_y // mesh.shape["col"], planes)
        classes = (mesh.shape["row"], mesh.shape["col"]) == (ROWS, COLS) and local == BLOCK
        return jax.shard_map(
            per_device_classes if classes else per_device,
            mesh=mesh,
            in_specs=placed,
            out_specs=(P("row", "col", None), P()),
            check_vma=False,
        )(density)

    return program
```

```python
import jax
import jax.numpy as jnp
from jax import lax
from jax.experimental import pallas as pl
from jax.experimental.pallas import tpu as pltpu
from jax.sharding import PartitionSpec as P

SUB = 256


SPLINE_TAPS = (0.0625, 0.25, 0.375, 0.25, 0.0625)
SPACINGS = (4, 8, 16)
EPSILON = 1e-06


def padded_2(block, sides, width):
    for axis, dim in sides:
        count = lax.axis_size(axis)
        forward = [(i, i + 1) for i in range(count - 1)]
        forward.append((count - 1, 0))
        backward = [(target, source) for source, target in forward]
        low = lax.ppermute(
            lax.slice_in_dim(block, block.shape[dim] - width, None, axis=dim), axis, forward
        )
        high = lax.ppermute(lax.slice_in_dim(block, 0, width, axis=dim), axis, backward)
        block = jnp.concatenate([low, block, high], axis=dim)
    return block


def holed_pass(padded, spacing, axis_number, length_out):
    summed = SPLINE_TAPS[0] * lax.slice_in_dim(padded, 0, length_out, axis=axis_number)
    for tap_index in (1, 2, 3, 4):
        portion = lax.slice_in_dim(
            padded, tap_index * spacing, tap_index * spacing + length_out, axis=axis_number
        )
        summed = summed + SPLINE_TAPS[tap_index] * portion
    return summed


def depth_pass(values_in, spacing):
    summed = SPLINE_TAPS[2] * values_in
    for tap_index in (0, 1, 3, 4):
        summed = summed + SPLINE_TAPS[tap_index] * jnp.roll(
            values_in, -(tap_index - 2) * spacing, axis=2
        )
    return summed


def moment_planes(detail):
    square = detail * detail
    return jnp.stack(
        [
            jnp.sum(jnp.abs(detail), axis=2),
            jnp.sum(square, axis=2),
            jnp.sum(square * detail, axis=2),
            jnp.sum(square * square, axis=2),
        ]
    )


def finish_table(table, planes):
    means = table / jnp.float32(SUB * SUB * planes)
    second = means[:, 1]
    third = means[:, 2] / (second + EPSILON) ** 1.5
    fourth = means[:, 3] / (second + EPSILON) ** 2
    return jnp.stack([means[:, 0], second, third, fourth], axis=1)


def per_device(density):
    size_x, size_y, planes = density.shape
    plane_list = []
    current = density
    for spacing in SPACINGS:
        rows_padded = padded_2(current, (("row", 0),), 2 * spacing)
        along_x = holed_pass(rows_padded, spacing, 0, size_x)
        cols_padded = padded_2(along_x, (("col", 1),), 2 * spacing)
        along_y = holed_pass(cols_padded, spacing, 1, size_y)
        smoother = depth_pass(along_y, spacing)
        plane_list.append(moment_planes(current - smoother))
        current = smoother
    planes_all = jnp.stack(plane_list)
    count_x = lax.axis_size("row") * size_x // SUB
    count_y = lax.axis_size("col") * size_y // SUB
    rows_global = lax.axis_index("row") * size_x + jnp.arange(size_x, dtype=jnp.int32)
    cols_global = lax.axis_index("col") * size_y + jnp.arange(size_y, dtype=jnp.int32)
    onehot_x = (
        (rows_global // SUB)[:, None] == jnp.arange(count_x, dtype=jnp.int32)[None, :]
    ).astype(jnp.float32)
    onehot_y = (
        (cols_global // SUB)[:, None] == jnp.arange(count_y, dtype=jnp.int32)[None, :]
    ).astype(jnp.float32)
    partial_table = jnp.einsum(
        "xa,skxy,yb->skab", onehot_x, planes_all, onehot_y, precision=lax.Precision.HIGHEST
    )
    table = lax.psum(partial_table, ("row", "col"))
    return (current, finish_table(table, planes))


MESH = pl.DeviceIdType.MESH
ROWS, COLS = 4, 8
DEVICES = ROWS * COLS
BLOCK = (64, 32, 128)
CLASS_X, CLASS_Y, LANES = 64, 64, 128
CHUNKS = 2


def five_taps(low2, low1, mid, high1, high2):
    return (
        SPLINE_TAPS[0] * (low2 + high2) + SPLINE_TAPS[1] * (low1 + high1) + SPLINE_TAPS[2] * mid
    )


def roll(v, shift, axis):
    shift = shift % v.shape[axis]
    return pltpu.roll(v, shift, axis) if shift else v


def exchange_pair(lane, distance, first, second):
    clear = (lane & distance) == 0
    return (
        jnp.where(clear, first, roll(second, distance, 2)),
        jnp.where(clear, roll(first, -distance, 2), second),
    )


def class_kernel(
    x_hbm,
    out_ref,
    tab_ref,
    x_ref,
    send,
    f0,
    f1,
    back,
    padded,
    taps,
    sums,
    ssem,
    rsem,
    bssem,
    brsem,
    mssem,
    mrsem,
    xsem,
):
    row, col = lax.axis_index("row"), lax.axis_index("col")
    me = row * COLS + col
    col_hi, col_lo = lax.div(col, 2), lax.rem(col, 2)

    order = jnp.where(
        col_hi == 0, 30, jnp.where(col_hi == 1, 180, jnp.where(col_hi == 2, 75, 225))
    )

    planes = [lax.rem(lax.div(order, 4**step), 4) for step in range(4)]

    def each_other(visit):
        for hi in planes:

            @pl.loop(0, ROWS)
            def _(near):
                r = row + near
                r = jnp.where(r >= ROWS, r - ROWS, r)
                visit(r, 2 * hi + 1 - col_lo)

                @pl.when(r * COLS + 2 * hi + col_lo != me)
                def _():
                    visit(r, 2 * hi + col_lo)

    def place(ref, h, r, c):
        return ref.at[h, 4 * r, c]

    def load_x(rx):
        return pltpu.make_async_copy(x_hbm.at[:, rx], x_ref.at[:, rx], xsem.at[rx])

    for rx in range(4):
        load_x(rx).start()

    barrier = pltpu.get_barrier_semaphore()

    each_other(
        lambda r, c: pl.semaphore_signal(
            barrier, inc=1, device_id=(r, c), device_id_type=MESH
        )
    )

    lane3 = lax.broadcasted_iota(jnp.int32, (4, 8, LANES), 2)

    def pack(h):
        @pl.loop(0, 4)
        def _(rx):
            if h == 0:
                load_x(rx).wait()
            for ry in range(4):
                v = [
                    jnp.stack([x_ref[4 * q + i, rx, pl.ds(ry, 8, stride=4), :] for i in range(4)])
                    for q in range(4)
                ]
                u0 = exchange_pair(lane3, 2, v[0], v[2])[h]
                u1 = exchange_pair(lane3, 2, v[1], v[3])[h]
                w0, w1 = exchange_pair(lane3, 1, u0, u1)
                send[h, rx * COLS + 2 * ry] = w0
                send[h, rx * COLS + 2 * ry + 1] = w1

    def forward(h, r, c, source_r, source_c):
        k = r * COLS + c
        return pltpu.make_async_remote_copy(
            src_ref=send.at[h, k],
            dst_ref=place(f0, h, source_r, source_c),
            send_sem=ssem.at[h, k],
            recv_sem=rsem.at[h, source_r * COLS + source_c],
            device_id=(r, c),
            device_id_type=MESH,
        )

    def send_all(h):
        each_other(lambda r, c: forward(h, r, c, row, col).start())
        f0[h, 4 * row, col] = send[h, me]

    def receive_all(h):
        each_other(lambda r, c: forward(h, r, c, r, c).wait_recv())

    lane2 = lax.broadcasted_iota(jnp.int32, (CLASS_Y, LANES), 1)
    lane = lax.broadcasted_iota(jnp.int32, (1, LANES), 1)

    def fill(ref, h, unit):
        for r in range(4):
            for i in range(4):
                here = ref[h, 4 * r, :, i].reshape(CLASS_Y, LANES)
                after = ref[h, 4 * ((r + 1) % 4), :, i].reshape(CLASS_Y, LANES)
                for m in (1, 2, 3):
                    reached = (i < 2 * unit, unit == 4, i >= 4 - 2 * unit)[m - 1]
                    if reached:
                        ref[h, 4 * r + m, :, i] = jnp.where(
                            (lane2 & 3) < 4 - m, roll(here, -m, 1), roll(after, 4 - m, 1)
                        ).reshape(8, 8, LANES)

    def make_taps():
        shape = (2 * LANES, LANES)
        gap = (
            lax.broadcasted_iota(jnp.int32, shape, 0) - lax.broadcasted_iota(jnp.int32, shape, 1)
        ) & (LANES - 1)
        for scale, spacing in enumerate(SPACINGS):
            matrix = jnp.zeros(shape, jnp.float32)
            for k, tap in zip(range(-2, 3), SPLINE_TAPS):
                matrix = jnp.where(gap == (k * spacing) % LANES, tap, matrix)
            taps[scale] = matrix.astype(jnp.bfloat16)

    def smooth_rows(src, dst, h, scale, r, acc):
        unit = SPACINGS[scale] // 4
        mids = []
        for i in range(4):

            def at(k):
                n = i + k * unit
                return src[h, (4 * r + n // 4) % 16, :, n % 4].reshape(CLASS_Y, LANES)

            mids.append(at(0))
            v = five_taps(at(-2), at(-1), mids[i], at(1), at(2))
            padded[i, 8:72, :] = v
            padded[i, 0:8, :] = v[56:]
            padded[i, 72:80, :] = v[:8]
        rows = []
        for i in range(4):
            rows.append(
                five_taps(*(padded[i, 8 + k * unit : 72 + k * unit, :] for k in range(-2, 3)))
            )
        v = jnp.concatenate(rows, axis=0)
        high = v.astype(jnp.bfloat16)
        low = (v - high.astype(jnp.float32)).astype(jnp.bfloat16)
        v = jnp.dot(
            jnp.concatenate([high, low], axis=1), taps[scale], preferred_element_type=jnp.float32
        )
        for i in range(4):
            smooth = v[CLASS_Y * i : CLASS_Y * (i + 1)]
            dst[h, 4 * r, :, i] = smooth.reshape(8, 8, LANES)
            detail = (mids[i] - smooth).reshape(8, 8, LANES)
            square = detail * detail
            parts = (jnp.abs(detail), square, square * detail, square * square)
            acc = tuple(s + jnp.sum(p, axis=0) for s, p in zip(acc, parts))
        return acc

    def backward(h, r, c, source_r, source_c):
        source = source_r * COLS + source_c
        return pltpu.make_async_remote_copy(
            src_ref=place(f1, h, r, c),
            dst_ref=back.at[h, source],
            send_sem=bssem.at[h, r * COLS + c],
            recv_sem=brsem.at[h, source],
            device_id=(r, c),
            device_id_type=MESH,
        )

    def scales(h, accs):
        fields = (f0, f1, f0, f1)
        results = []
        for scale, spacing in enumerate(SPACINGS):
            src, dst = fields[scale], fields[scale + 1]
            fill(src, h, spacing // 4)

            acc = accs[scale]
            for r in range(4):
                acc = smooth_rows(src, dst, h, scale, r, acc)
            results.append(acc)
        each_other(lambda r, c: backward(h, r, c, row, col).start())
        back[h, me] = f1[h, 4 * row, col]
        return results

    make_taps()
    pack(0)
    pl.semaphore_wait(barrier, DEVICES - 1)
    send_all(0)
    pack(1)
    send_all(1)
    accs = [(jnp.zeros((8, LANES), jnp.float32),) * 4] * len(SPACINGS)

    def chunk(h, accs):
        receive_all(h)
        return scales(h, accs)

    accs = lax.fori_loop(0, CHUNKS, chunk, accs)

    total = jnp.zeros((1, LANES), jnp.float32)
    for scale, acc in enumerate(accs):
        for moment, s in enumerate(acc):
            value = jnp.sum(jnp.sum(s, axis=0, keepdims=True), axis=1, keepdims=True)
            total = total + jnp.where(lane == 4 * scale + moment, value, 0.0)
    sums[me] = total

    def share(r, c, source):
        return pltpu.make_async_remote_copy(
            src_ref=sums.at[me],
            dst_ref=sums.at[source],
            send_sem=mssem.at[r * COLS + c],
            recv_sem=mrsem.at[source],
            device_id=(r, c),
            device_id_type=MESH,
        )

    each_other(lambda r, c: share(r, c, me).start())

    @pl.loop(0, 4)
    def _(j):
        rx = lax.rem(row + 4 - j, 4)
        for ry in range(4):
            u = []
            for h in range(CHUNKS):
                for p in range(2):
                    c = 2 * ry + p

                    @pl.when(rx * COLS + c != me)
                    def _():
                        backward(h, rx, c, rx, c).wait_recv()

                u.append(
                    exchange_pair(
                        lane3, 1, back[h, rx * COLS + 2 * ry], back[h, rx * COLS + 2 * ry + 1]
                    )
                )
            for q in range(2):
                for low, v in enumerate(exchange_pair(lane3, 2, u[0][q], u[1][q])):
                    for i in range(4):
                        out_ref[4 * (q + 2 * low) + i, rx, pl.ds(ry, 8, stride=4), :] = v[i]

    def finish(r, c):
        share(r, c, r * COLS + c).wait_recv()
        share(r, c, r * COLS + c).wait_send()
        for h in range(CHUNKS):
            forward(h, r, c, r, c).wait_send()
            backward(h, r, c, r, c).wait_send()

    each_other(finish)

    tab_ref[...] = jnp.sum(sums[...], axis=0)


def per_device_classes(density):
    size_x, size_y, planes = density.shape
    dma = pltpu.SemaphoreType.DMA((CHUNKS, DEVICES))
    one = pltpu.SemaphoreType.DMA((DEVICES,))
    block = pltpu.VMEM((CHUNKS, DEVICES, 4, 8, LANES), jnp.float32)
    field = pltpu.VMEM((CHUNKS, CLASS_X // 4, CLASS_Y // 8, 4, 8, LANES), jnp.float32)
    coarse, sums = pl.pallas_call(
        class_kernel,
        out_shape=(
            jax.ShapeDtypeStruct((16, 4, size_y, planes), jnp.float32),
            jax.ShapeDtypeStruct((1, LANES), jnp.float32),
        ),
        in_specs=[pl.BlockSpec(memory_space=pltpu.HBM)],
        out_specs=(pl.BlockSpec(memory_space=pltpu.VMEM),) * 2,
        scratch_shapes=[
            pltpu.VMEM((16, 4, size_y, planes), jnp.float32),
            block,
            field,
            field,
            block,
            pltpu.VMEM((4, CLASS_Y + 16, LANES), jnp.float32),
            pltpu.VMEM((len(SPACINGS), 2 * LANES, LANES), jnp.bfloat16),
            pltpu.VMEM((DEVICES, 1, LANES), jnp.float32),
        ]
        + [dma] * 4
        + [one] * 2
        + [pltpu.SemaphoreType.DMA((4,))],
        compiler_params=pltpu.CompilerParams(
            collective_id=0, has_side_effects=True, vmem_limit_bytes=32 * 1024 * 1024
        ),
    )(density.reshape(16, 4, size_y, planes))
    table = sums[0, :12].reshape(3, 4, 1, 1)
    return coarse.reshape(size_x, size_y, planes), finish_table(table, planes)


def solution(mesh):
    placed = (P("row", "col", None),)

    def program(density):
        size_x, size_y, planes = density.shape
        local = (size_x // mesh.shape["row"], size_y // mesh.shape["col"], planes)
        classes = (mesh.shape["row"], mesh.shape["col"]) == (ROWS, COLS) and local == BLOCK
        return jax.shard_map(
            per_device_classes if classes else per_device,
            mesh=mesh,
            in_specs=placed,
            out_specs=(P("row", "col", None), P()),
            check_vma=False,
        )(density)

    return program
```

```python
import jax
import jax.numpy as jnp
from jax import lax
from jax.experimental import pallas as pl
from jax.experimental.pallas import tpu as pltpu
from jax.sharding import PartitionSpec as P

SUB = 256


SPLINE_TAPS = (0.0625, 0.25, 0.375, 0.25, 0.0625)
SPACINGS = (4, 8, 16)
EPSILON = 1e-06


def padded_2(block, sides, width):
    for axis, dim in sides:
        count = lax.axis_size(axis)
        forward = [(i, i + 1) for i in range(count - 1)]
        forward.append((count - 1, 0))
        backward = [(target, source) for source, target in forward]
        low = lax.ppermute(
            lax.slice_in_dim(block, block.shape[dim] - width, None, axis=dim), axis, forward
        )
        high = lax.ppermute(lax.slice_in_dim(block, 0, width, axis=dim), axis, backward)
        block = jnp.concatenate([low, block, high], axis=dim)
    return block


def holed_pass(padded, spacing, axis_number, length_out):
    summed = SPLINE_TAPS[0] * lax.slice_in_dim(padded, 0, length_out, axis=axis_number)
    for tap_index in (1, 2, 3, 4):
        portion = lax.slice_in_dim(
            padded, tap_index * spacing, tap_index * spacing + length_out, axis=axis_number
        )
        summed = summed + SPLINE_TAPS[tap_index] * portion
    return summed


def depth_pass(values_in, spacing):
    summed = SPLINE_TAPS[2] * values_in
    for tap_index in (0, 1, 3, 4):
        summed = summed + SPLINE_TAPS[tap_index] * jnp.roll(
            values_in, -(tap_index - 2) * spacing, axis=2
        )
    return summed


def moment_planes(detail):
    square = detail * detail
    return jnp.stack(
        [
            jnp.sum(jnp.abs(detail), axis=2),
            jnp.sum(square, axis=2),
            jnp.sum(square * detail, axis=2),
            jnp.sum(square * square, axis=2),
        ]
    )


def finish_table(table, planes):
    means = table / jnp.float32(SUB * SUB * planes)
    second = means[:, 1]
    third = means[:, 2] / (second + EPSILON) ** 1.5
    fourth = means[:, 3] / (second + EPSILON) ** 2
    return jnp.stack([means[:, 0], second, third, fourth], axis=1)


def per_device(density):
    size_x, size_y, planes = density.shape
    plane_list = []
    current = density
    for spacing in SPACINGS:
        rows_padded = padded_2(current, (("row", 0),), 2 * spacing)
        along_x = holed_pass(rows_padded, spacing, 0, size_x)
        cols_padded = padded_2(along_x, (("col", 1),), 2 * spacing)
        along_y = holed_pass(cols_padded, spacing, 1, size_y)
        smoother = depth_pass(along_y, spacing)
        plane_list.append(moment_planes(current - smoother))
        current = smoother
    planes_all = jnp.stack(plane_list)
    count_x = lax.axis_size("row") * size_x // SUB
    count_y = lax.axis_size("col") * size_y // SUB
    rows_global = lax.axis_index("row") * size_x + jnp.arange(size_x, dtype=jnp.int32)
    cols_global = lax.axis_index("col") * size_y + jnp.arange(size_y, dtype=jnp.int32)
    onehot_x = (
        (rows_global // SUB)[:, None] == jnp.arange(count_x, dtype=jnp.int32)[None, :]
    ).astype(jnp.float32)
    onehot_y = (
        (cols_global // SUB)[:, None] == jnp.arange(count_y, dtype=jnp.int32)[None, :]
    ).astype(jnp.float32)
    partial_table = jnp.einsum(
        "xa,skxy,yb->skab", onehot_x, planes_all, onehot_y, precision=lax.Precision.HIGHEST
    )
    table = lax.psum(partial_table, ("row", "col"))
    return (current, finish_table(table, planes))


MESH = pl.DeviceIdType.MESH
ROWS, COLS = 4, 8
DEVICES = ROWS * COLS
BLOCK = (64, 32, 128)
CLASS_X, CLASS_Y, LANES = 64, 64, 128
CHUNKS = 2


def five_taps(low2, low1, mid, high1, high2):
    return (
        SPLINE_TAPS[0] * (low2 + high2) + SPLINE_TAPS[1] * (low1 + high1) + SPLINE_TAPS[2] * mid
    )


def roll(v, shift, axis):
    shift = shift % v.shape[axis]
    return pltpu.roll(v, shift, axis) if shift else v


def exchange_pair(lane, distance, first, second):
    clear = (lane & distance) == 0
    return (
        jnp.where(clear, first, roll(second, distance, 2)),
        jnp.where(clear, roll(first, -distance, 2), second),
    )


def class_kernel(
    x_hbm,
    out_hbm,
    tab_ref,
    x_ref,
    out_ref,
    send,
    f0,
    f1,
    back,
    padded,
    taps,
    sums,
    ssem,
    rsem,
    bssem,
    brsem,
    mssem,
    mrsem,
    xsem,
    osem,
):
    row, col = lax.axis_index("row"), lax.axis_index("col")
    me = row * COLS + col
    col_hi, col_lo = lax.div(col, 2), lax.rem(col, 2)

    order = jnp.where(
        col_hi == 0, 30, jnp.where(col_hi == 1, 180, jnp.where(col_hi == 2, 75, 225))
    )

    planes = [lax.rem(lax.div(order, 4**step), 4) for step in range(4)]

    def each_other(visit):
        for hi in planes:

            @pl.loop(0, ROWS)
            def _(near):
                r = row + near
                r = jnp.where(r >= ROWS, r - ROWS, r)
                visit(r, 2 * hi + 1 - col_lo)

                @pl.when(r * COLS + 2 * hi + col_lo != me)
                def _():
                    visit(r, 2 * hi + col_lo)

    def place(ref, h, r, c):
        return ref.at[h, 4 * r, c]

    def load_x(rx):
        return pltpu.make_async_copy(x_hbm.at[:, rx], x_ref.at[:, rx], xsem.at[rx])

    def store_out(rx):
        return pltpu.make_async_copy(out_ref.at[:, rx], out_hbm.at[:, rx], osem.at[rx])

    for rx in range(4):
        load_x(rx).start()

    barrier = pltpu.get_barrier_semaphore()

    each_other(
        lambda r, c: pl.semaphore_signal(
            barrier, inc=1, device_id=(r, c), device_id_type=MESH
        )
    )

    lane3 = lax.broadcasted_iota(jnp.int32, (4, 8, LANES), 2)

    def pack(h):
        @pl.loop(0, 4)
        def _(rx):
            if h == 0:
                load_x(rx).wait()
            for ry in range(4):
                v = [
                    jnp.stack([x_ref[4 * q + i, rx, pl.ds(ry, 8, stride=4), :] for i in range(4)])
                    for q in range(4)
                ]
                u0 = exchange_pair(lane3, 2, v[0], v[2])[h]
                u1 = exchange_pair(lane3, 2, v[1], v[3])[h]
                w0, w1 = exchange_pair(lane3, 1, u0, u1)
                send[h, rx * COLS + 2 * ry] = w0
                send[h, rx * COLS + 2 * ry + 1] = w1

    def forward(h, r, c, source_r, source_c):
        k = r * COLS + c
        return pltpu.make_async_remote_copy(
            src_ref=send.at[h, k],
            dst_ref=place(f0, h, source_r, source_c),
            send_sem=ssem.at[h],
            recv_sem=rsem.at[h],
            device_id=(r, c),
            device_id_type=MESH,
        )

    def send_all(h):
        each_other(lambda r, c: forward(h, r, c, row, col).start())
        f0[h, 4 * row, col] = send[h, me]

    def wait_bytes(ref, sem):
        pltpu.make_async_copy(ref, ref, sem).wait()

    others = pl.ds(0, DEVICES - 1)

    lane2 = lax.broadcasted_iota(jnp.int32, (CLASS_Y, LANES), 1)
    lane = lax.broadcasted_iota(jnp.int32, (1, LANES), 1)

    def fill(ref, h, unit):
        for r in range(4):
            for i in range(4):
                here = ref[h, 4 * r, :, i].reshape(CLASS_Y, LANES)
                after = ref[h, 4 * ((r + 1) % 4), :, i].reshape(CLASS_Y, LANES)
                for m in (1, 2, 3):
                    reached = (i < 2 * unit, unit == 4, i >= 4 - 2 * unit)[m - 1]
                    if reached:
                        ref[h, 4 * r + m, :, i] = jnp.where(
                            (lane2 & 3) < 4 - m, roll(here, -m, 1), roll(after, 4 - m, 1)
                        ).reshape(8, 8, LANES)

    def make_taps():
        shape = (2 * LANES, LANES)
        gap = (
            lax.broadcasted_iota(jnp.int32, shape, 0) - lax.broadcasted_iota(jnp.int32, shape, 1)
        ) & (LANES - 1)
        for scale, spacing in enumerate(SPACINGS):
            matrix = jnp.zeros(shape, jnp.float32)
            for k, tap in zip(range(-2, 3), SPLINE_TAPS):
                matrix = jnp.where(gap == (k * spacing) % LANES, tap, matrix)
            taps[scale] = matrix.astype(jnp.bfloat16)

    def smooth_rows(src, dst, h, scale, r, acc):
        unit = SPACINGS[scale] // 4
        mids = []
        for i in range(4):

            def at(k):
                n = i + k * unit
                return src[h, (4 * r + n // 4) % 16, :, n % 4].reshape(CLASS_Y, LANES)

            mids.append(at(0))
            v = five_taps(at(-2), at(-1), mids[i], at(1), at(2))
            padded[i, 8:72, :] = v
            padded[i, 0:8, :] = v[56:]
            padded[i, 72:80, :] = v[:8]
        rows = []
        for i in range(4):
            rows.append(
                five_taps(*(padded[i, 8 + k * unit : 72 + k * unit, :] for k in range(-2, 3)))
            )
        v = jnp.concatenate(rows, axis=0)
        high = v.astype(jnp.bfloat16)
        low = (v - high.astype(jnp.float32)).astype(jnp.bfloat16)
        v = jnp.dot(
            jnp.concatenate([high, low], axis=1), taps[scale], preferred_element_type=jnp.float32
        )
        for i in range(4):
            smooth = v[CLASS_Y * i : CLASS_Y * (i + 1)]
            dst[h, 4 * r, :, i] = smooth.reshape(8, 8, LANES)
            detail = (mids[i] - smooth).reshape(8, 8, LANES)
            square = detail * detail
            parts = (jnp.abs(detail), square, square * detail, square * square)
            acc = tuple(s + jnp.sum(p, axis=0) for s, p in zip(acc, parts))
        return acc

    def backward(h, r, c, source_r, source_c):
        source = source_r * COLS + source_c
        return pltpu.make_async_remote_copy(
            src_ref=place(f1, h, r, c),
            dst_ref=back.at[h, source],
            send_sem=bssem.at[h],
            recv_sem=brsem.at[h, source_r],
            device_id=(r, c),
            device_id_type=MESH,
        )

    def scales(h, accs):
        fields = (f0, f1, f0, f1)
        results = []
        for scale, spacing in enumerate(SPACINGS):
            src, dst = fields[scale], fields[scale + 1]
            fill(src, h, spacing // 4)

            acc = accs[scale]
            for r in range(4):
                acc = smooth_rows(src, dst, h, scale, r, acc)
            results.append(acc)
        each_other(lambda r, c: backward(h, r, c, row, col).start())
        back[h, me] = f1[h, 4 * row, col]
        return results

    make_taps()
    pack(0)
    pl.semaphore_wait(barrier, DEVICES - 1)
    send_all(0)
    pack(1)
    send_all(1)
    accs = [(jnp.zeros((8, LANES), jnp.float32),) * 4] * len(SPACINGS)

    def chunk(h, accs):
        wait_bytes(send.at[h, others], rsem.at[h])
        return scales(h, accs)

    accs = lax.fori_loop(0, CHUNKS, chunk, accs)

    total = jnp.zeros((1, LANES), jnp.float32)
    for scale, acc in enumerate(accs):
        for moment, s in enumerate(acc):
            value = jnp.sum(jnp.sum(s, axis=0, keepdims=True), axis=1, keepdims=True)
            total = total + jnp.where(lane == 4 * scale + moment, value, 0.0)
    sums[me] = total

    def share(r, c, source):
        return pltpu.make_async_remote_copy(
            src_ref=sums.at[me],
            dst_ref=sums.at[source],
            send_sem=mssem,
            recv_sem=mrsem,
            device_id=(r, c),
            device_id_type=MESH,
        )

    each_other(lambda r, c: share(r, c, me).start())

    @pl.loop(0, 4)
    def _(j):
        rx = lax.rem(row + 4 - j, 4)
        for h in range(CHUNKS):

            @pl.when(rx == row)
            def _():
                wait_bytes(send.at[h, pl.ds(0, COLS - 1)], brsem.at[h, rx])

            @pl.when(rx != row)
            def _():
                wait_bytes(send.at[h, pl.ds(0, COLS)], brsem.at[h, rx])

        for ry in range(4):
            u = []
            for h in range(CHUNKS):
                u.append(
                    exchange_pair(
                        lane3, 1, back[h, rx * COLS + 2 * ry], back[h, rx * COLS + 2 * ry + 1]
                    )
                )
            for q in range(2):
                for low, v in enumerate(exchange_pair(lane3, 2, u[0][q], u[1][q])):
                    for i in range(4):
                        out_ref[4 * (q + 2 * low) + i, rx, pl.ds(ry, 8, stride=4), :] = v[i]
        store_out(rx).start()

    wait_bytes(sums.at[others], mrsem)
    wait_bytes(sums.at[others], mssem)
    for h in range(CHUNKS):
        wait_bytes(send.at[h, others], ssem.at[h])
        wait_bytes(send.at[h, others], bssem.at[h])

    tab_ref[...] = jnp.sum(sums[...], axis=0)
    for rx in range(4):
        store_out(rx).wait()


def per_device_classes(density):
    size_x, size_y, planes = density.shape
    dma = pltpu.SemaphoreType.DMA((CHUNKS,))
    block = pltpu.VMEM((CHUNKS, DEVICES, 4, 8, LANES), jnp.float32)
    field = pltpu.VMEM((CHUNKS, CLASS_X // 4, CLASS_Y // 8, 4, 8, LANES), jnp.float32)
    coarse, sums = pl.pallas_call(
        class_kernel,
        out_shape=(
            jax.ShapeDtypeStruct((16, 4, size_y, planes), jnp.float32),
            jax.ShapeDtypeStruct((1, LANES), jnp.float32),
        ),
        in_specs=[pl.BlockSpec(memory_space=pltpu.HBM)],
        out_specs=(
            pl.BlockSpec(memory_space=pltpu.HBM),
            pl.BlockSpec(memory_space=pltpu.VMEM),
        ),
        scratch_shapes=[
            pltpu.VMEM((16, 4, size_y, planes), jnp.float32),
            pltpu.VMEM((16, 4, size_y, planes), jnp.float32),
            block,
            field,
            field,
            block,
            pltpu.VMEM((4, CLASS_Y + 16, LANES), jnp.float32),
            pltpu.VMEM((len(SPACINGS), 2 * LANES, LANES), jnp.bfloat16),
            pltpu.VMEM((DEVICES, 1, LANES), jnp.float32),
        ]
        + [dma] * 3
        + [pltpu.SemaphoreType.DMA((CHUNKS, ROWS))]
        + [pltpu.SemaphoreType.DMA] * 2
        + [pltpu.SemaphoreType.DMA((4,))] * 2,
        compiler_params=pltpu.CompilerParams(
            collective_id=0, has_side_effects=True, vmem_limit_bytes=60 * 1024 * 1024
        ),
    )(density.reshape(16, 4, size_y, planes))
    table = sums[0, :12].reshape(3, 4, 1, 1)
    return coarse.reshape(size_x, size_y, planes), finish_table(table, planes)


def solution(mesh):
    placed = (P("row", "col", None),)

    def program(density):
        size_x, size_y, planes = density.shape
        local = (size_x // mesh.shape["row"], size_y // mesh.shape["col"], planes)
        classes = (mesh.shape["row"], mesh.shape["col"]) == (ROWS, COLS) and local == BLOCK
        return jax.shard_map(
            per_device_classes if classes else per_device,
            mesh=mesh,
            in_specs=placed,
            out_specs=(P("row", "col", None), P()),
            check_vma=False,
        )(density)

    return program
```

```python
import jax
import jax.numpy as jnp
from jax import lax
from jax.experimental import pallas as pl
from jax.experimental.pallas import tpu as pltpu
from jax.sharding import PartitionSpec as P

SUB = 256


SPLINE_TAPS = (0.0625, 0.25, 0.375, 0.25, 0.0625)
SPACINGS = (4, 8, 16)
EPSILON = 1e-06


def padded_2(block, sides, width):
    for axis, dim in sides:
        count = lax.axis_size(axis)
        forward = [(i, i + 1) for i in range(count - 1)]
        forward.append((count - 1, 0))
        backward = [(target, source) for source, target in forward]
        low = lax.ppermute(
            lax.slice_in_dim(block, block.shape[dim] - width, None, axis=dim), axis, forward
        )
        high = lax.ppermute(lax.slice_in_dim(block, 0, width, axis=dim), axis, backward)
        block = jnp.concatenate([low, block, high], axis=dim)
    return block


def holed_pass(padded, spacing, axis_number, length_out):
    summed = SPLINE_TAPS[0] * lax.slice_in_dim(padded, 0, length_out, axis=axis_number)
    for tap_index in (1, 2, 3, 4):
        portion = lax.slice_in_dim(
            padded, tap_index * spacing, tap_index * spacing + length_out, axis=axis_number
        )
        summed = summed + SPLINE_TAPS[tap_index] * portion
    return summed


def depth_pass(values_in, spacing):
    summed = SPLINE_TAPS[2] * values_in
    for tap_index in (0, 1, 3, 4):
        summed = summed + SPLINE_TAPS[tap_index] * jnp.roll(
            values_in, -(tap_index - 2) * spacing, axis=2
        )
    return summed


def moment_planes(detail):
    square = detail * detail
    return jnp.stack(
        [
            jnp.sum(jnp.abs(detail), axis=2),
            jnp.sum(square, axis=2),
            jnp.sum(square * detail, axis=2),
            jnp.sum(square * square, axis=2),
        ]
    )


def finish_table(table, planes):
    means = table / jnp.float32(SUB * SUB * planes)
    second = means[:, 1]
    third = means[:, 2] / (second + EPSILON) ** 1.5
    fourth = means[:, 3] / (second + EPSILON) ** 2
    return jnp.stack([means[:, 0], second, third, fourth], axis=1)


def per_device(density):
    size_x, size_y, planes = density.shape
    plane_list = []
    current = density
    for spacing in SPACINGS:
        rows_padded = padded_2(current, (("row", 0),), 2 * spacing)
        along_x = holed_pass(rows_padded, spacing, 0, size_x)
        cols_padded = padded_2(along_x, (("col", 1),), 2 * spacing)
        along_y = holed_pass(cols_padded, spacing, 1, size_y)
        smoother = depth_pass(along_y, spacing)
        plane_list.append(moment_planes(current - smoother))
        current = smoother
    planes_all = jnp.stack(plane_list)
    count_x = lax.axis_size("row") * size_x // SUB
    count_y = lax.axis_size("col") * size_y // SUB
    rows_global = lax.axis_index("row") * size_x + jnp.arange(size_x, dtype=jnp.int32)
    cols_global = lax.axis_index("col") * size_y + jnp.arange(size_y, dtype=jnp.int32)
    onehot_x = (
        (rows_global // SUB)[:, None] == jnp.arange(count_x, dtype=jnp.int32)[None, :]
    ).astype(jnp.float32)
    onehot_y = (
        (cols_global // SUB)[:, None] == jnp.arange(count_y, dtype=jnp.int32)[None, :]
    ).astype(jnp.float32)
    partial_table = jnp.einsum(
        "xa,skxy,yb->skab", onehot_x, planes_all, onehot_y, precision=lax.Precision.HIGHEST
    )
    table = lax.psum(partial_table, ("row", "col"))
    return (current, finish_table(table, planes))


MESH = pl.DeviceIdType.MESH
ROWS, COLS = 4, 8
DEVICES = ROWS * COLS
BLOCK = (64, 32, 128)
CLASS_X, CLASS_Y, LANES = 64, 64, 128
CHUNKS = 2


def five_taps(low2, low1, mid, high1, high2):
    return (
        SPLINE_TAPS[0] * (low2 + high2) + SPLINE_TAPS[1] * (low1 + high1) + SPLINE_TAPS[2] * mid
    )


def roll(v, shift, axis):
    shift = shift % v.shape[axis]
    return pltpu.roll(v, shift, axis) if shift else v


def exchange_pair(lane, distance, first, second):
    clear = (lane & distance) == 0
    return (
        jnp.where(clear, first, roll(second, distance, 2)),
        jnp.where(clear, roll(first, -distance, 2), second),
    )


def class_kernel(
    x_hbm,
    out_ref,
    tab_ref,
    x_ref,
    send,
    f0,
    f1,
    back,
    padded,
    taps,
    sums,
    ssem,
    rsem,
    bssem,
    brsem,
    mssem,
    mrsem,
    xsem,
):
    row, col = lax.axis_index("row"), lax.axis_index("col")
    me = row * COLS + col
    col_hi, col_lo = lax.div(col, 2), lax.rem(col, 2)

    order = jnp.where(
        col_hi == 0, 30, jnp.where(col_hi == 1, 180, jnp.where(col_hi == 2, 75, 225))
    )

    planes = [lax.rem(lax.div(order, 4**step), 4) for step in range(4)]

    def each_other(visit):
        for hi in planes:

            @pl.loop(0, ROWS)
            def _(near):
                r = row + near
                r = jnp.where(r >= ROWS, r - ROWS, r)
                visit(r, 2 * hi + 1 - col_lo)

                @pl.when(r * COLS + 2 * hi + col_lo != me)
                def _():
                    visit(r, 2 * hi + col_lo)

    def place(ref, h, r, c):
        return ref.at[h, 4 * r, c]

    def load_x(rx):
        return pltpu.make_async_copy(x_hbm.at[:, rx], x_ref.at[:, rx], xsem.at[rx])

    for rx in range(4):
        load_x(rx).start()

    barrier = pltpu.get_barrier_semaphore()

    each_other(
        lambda r, c: pl.semaphore_signal(
            barrier, inc=1, device_id=(r, c), device_id_type=MESH
        )
    )

    lane3 = lax.broadcasted_iota(jnp.int32, (4, 8, LANES), 2)

    def pack(h):
        @pl.loop(0, 4)
        def _(rx):
            if h == 0:
                load_x(rx).wait()
            for ry in range(4):
                v = [
                    jnp.stack([x_ref[4 * q + i, rx, pl.ds(ry, 8, stride=4), :] for i in range(4)])
                    for q in range(4)
                ]
                u0 = exchange_pair(lane3, 2, v[0], v[2])[h]
                u1 = exchange_pair(lane3, 2, v[1], v[3])[h]
                w0, w1 = exchange_pair(lane3, 1, u0, u1)
                send[h, rx * COLS + 2 * ry] = w0
                send[h, rx * COLS + 2 * ry + 1] = w1

    def forward(h, r, c, source_r, source_c):
        k = r * COLS + c
        return pltpu.make_async_remote_copy(
            src_ref=send.at[h, k],
            dst_ref=place(f0, h, source_r, source_c),
            send_sem=ssem.at[h],
            recv_sem=rsem.at[h],
            device_id=(r, c),
            device_id_type=MESH,
        )

    def send_all(h):
        each_other(lambda r, c: forward(h, r, c, row, col).start())
        f0[h, 4 * row, col] = send[h, me]

    def wait_bytes(ref, sem):
        pltpu.make_async_copy(ref, ref, sem).wait()

    others = pl.ds(0, DEVICES - 1)

    lane2 = lax.broadcasted_iota(jnp.int32, (CLASS_Y, LANES), 1)
    lane = lax.broadcasted_iota(jnp.int32, (1, LANES), 1)

    def fill(ref, h, unit):
        for r in range(4):
            for i in range(4):
                here = ref[h, 4 * r, :, i].reshape(CLASS_Y, LANES)
                after = ref[h, 4 * ((r + 1) % 4), :, i].reshape(CLASS_Y, LANES)
                for m in (1, 2, 3):
                    reached = (i < 2 * unit, unit == 4, i >= 4 - 2 * unit)[m - 1]
                    if reached:
                        ref[h, 4 * r + m, :, i] = jnp.where(
                            (lane2 & 3) < 4 - m, roll(here, -m, 1), roll(after, 4 - m, 1)
                        ).reshape(8, 8, LANES)

    def make_taps():
        shape = (2 * LANES, LANES)
        gap = (
            lax.broadcasted_iota(jnp.int32, shape, 0) - lax.broadcasted_iota(jnp.int32, shape, 1)
        ) & (LANES - 1)
        for scale, spacing in enumerate(SPACINGS):
            matrix = jnp.zeros(shape, jnp.float32)
            for k, tap in zip(range(-2, 3), SPLINE_TAPS):
                matrix = jnp.where(gap == (k * spacing) % LANES, tap, matrix)
            taps[scale] = matrix.astype(jnp.bfloat16)

    def smooth_rows(src, dst, h, scale, r, acc):
        unit = SPACINGS[scale] // 4
        mids = []
        for i in range(4):

            def at(k):
                n = i + k * unit
                block = 4 * r + n // 4
                block = jnp.where(block < 0, block + 16, jnp.where(block >= 16, block - 16, block))
                return src[h, block, :, n % 4].reshape(CLASS_Y, LANES)

            mids.append(at(0))
            v = five_taps(at(-2), at(-1), mids[i], at(1), at(2))
            padded[i, 8:72, :] = v
            padded[i, 0:8, :] = v[56:]
            padded[i, 72:80, :] = v[:8]
        rows = []
        for i in range(4):
            rows.append(
                five_taps(*(padded[i, 8 + k * unit : 72 + k * unit, :] for k in range(-2, 3)))
            )
        v = jnp.concatenate(rows, axis=0)
        high = v.astype(jnp.bfloat16)
        low = (v - high.astype(jnp.float32)).astype(jnp.bfloat16)
        v = jnp.dot(
            jnp.concatenate([high, low], axis=1), taps[scale], preferred_element_type=jnp.float32
        )
        for i in range(4):
            smooth = v[CLASS_Y * i : CLASS_Y * (i + 1)]
            dst[h, 4 * r, :, i] = smooth.reshape(8, 8, LANES)
            detail = (mids[i] - smooth).reshape(8, 8, LANES)
            square = detail * detail
            parts = (jnp.abs(detail), square, square * detail, square * square)
            acc = tuple(s + jnp.sum(p, axis=0) for s, p in zip(acc, parts))
        return acc

    def backward(h, r, c, source_r, source_c):
        source = source_r * COLS + source_c
        return pltpu.make_async_remote_copy(
            src_ref=place(f1, h, r, c),
            dst_ref=back.at[h, source],
            send_sem=bssem.at[h],
            recv_sem=brsem.at[h, source_r],
            device_id=(r, c),
            device_id_type=MESH,
        )

    def scales(h, accs):
        fields = (f0, f1, f0, f1)
        results = []
        for scale, spacing in enumerate(SPACINGS):
            src, dst = fields[scale], fields[scale + 1]
            fill(src, h, spacing // 4)

            acc = accs[scale]
            for near in range(4):
                r = row + near
                r = jnp.where(r >= ROWS, r - ROWS, r)
                acc = smooth_rows(src, dst, h, scale, r, acc)
                if scale == len(SPACINGS) - 1:
                    for hi in planes:
                        for c in (2 * hi + 1 - col_lo, 2 * hi + col_lo):

                            @pl.when(r * COLS + c != me)
                            def _():
                                backward(h, r, c, row, col).start()

            results.append(acc)
        back[h, me] = f1[h, 4 * row, col]
        return results

    make_taps()
    pack(0)
    pl.semaphore_wait(barrier, DEVICES - 1)
    send_all(0)
    pack(1)
    send_all(1)
    accs = [(jnp.zeros((8, LANES), jnp.float32),) * 4] * len(SPACINGS)

    def chunk(h, accs):
        wait_bytes(send.at[h, others], rsem.at[h])
        return scales(h, accs)

    accs = lax.fori_loop(0, CHUNKS, chunk, accs)

    total = jnp.zeros((1, LANES), jnp.float32)
    for scale, acc in enumerate(accs):
        for moment, s in enumerate(acc):
            value = jnp.sum(jnp.sum(s, axis=0, keepdims=True), axis=1, keepdims=True)
            total = total + jnp.where(lane == 4 * scale + moment, value, 0.0)
    sums[me] = total

    def share(r, c, source):
        return pltpu.make_async_remote_copy(
            src_ref=sums.at[me],
            dst_ref=sums.at[source],
            send_sem=mssem,
            recv_sem=mrsem,
            device_id=(r, c),
            device_id_type=MESH,
        )

    each_other(lambda r, c: share(r, c, me).start())

    @pl.loop(0, 4)
    def _(j):
        rx = lax.rem(row + 4 - j, 4)
        for h in range(CHUNKS):

            @pl.when(rx == row)
            def _():
                wait_bytes(send.at[h, pl.ds(0, COLS - 1)], brsem.at[h, rx])

            @pl.when(rx != row)
            def _():
                wait_bytes(send.at[h, pl.ds(0, COLS)], brsem.at[h, rx])

        for ry in range(4):
            u = []
            for h in range(CHUNKS):
                u.append(
                    exchange_pair(
                        lane3, 1, back[h, rx * COLS + 2 * ry], back[h, rx * COLS + 2 * ry + 1]
                    )
                )
            for q in range(2):
                for low, v in enumerate(exchange_pair(lane3, 2, u[0][q], u[1][q])):
                    for i in range(4):
                        out_ref[4 * (q + 2 * low) + i, rx, pl.ds(ry, 8, stride=4), :] = v[i]

    wait_bytes(sums.at[others], mrsem)
    wait_bytes(sums.at[others], mssem)
    for h in range(CHUNKS):
        wait_bytes(send.at[h, others], ssem.at[h])
        wait_bytes(send.at[h, others], bssem.at[h])

    means = jnp.sum(sums[...], axis=0) / jnp.float32(SUB * SUB * LANES)
    moment = lane & 3
    second = jnp.where(moment == 2, roll(means, 1, 1), roll(means, 2, 1)) + EPSILON
    power = second * jnp.where(moment == 2, jnp.sqrt(second), second)
    final = jnp.where(moment < 2, means, means / power)
    for scale in range(len(SPACINGS)):
        tab_ref[scale] = final[:, 4 * scale : 4 * scale + 4]


def per_device_classes(density):
    size_x, size_y, planes = density.shape
    dma = pltpu.SemaphoreType.DMA((CHUNKS,))
    block = pltpu.VMEM((CHUNKS, DEVICES, 4, 8, LANES), jnp.float32)
    field = pltpu.VMEM((CHUNKS, CLASS_X // 4, CLASS_Y // 8, 4, 8, LANES), jnp.float32)
    coarse, moments = pl.pallas_call(
        class_kernel,
        out_shape=(
            jax.ShapeDtypeStruct((16, 4, size_y, planes), jnp.float32),
            jax.ShapeDtypeStruct((len(SPACINGS), 1, 4), jnp.float32),
        ),
        in_specs=[pl.BlockSpec(memory_space=pltpu.HBM)],
        out_specs=(pl.BlockSpec(memory_space=pltpu.VMEM),) * 2,
        scratch_shapes=[
            pltpu.VMEM((16, 4, size_y, planes), jnp.float32),
            block,
            field,
            field,
            block,
            pltpu.VMEM((4, CLASS_Y + 16, LANES), jnp.float32),
            pltpu.VMEM((len(SPACINGS), 2 * LANES, LANES), jnp.bfloat16),
            pltpu.VMEM((DEVICES, 1, LANES), jnp.float32),
        ]
        + [dma] * 3
        + [pltpu.SemaphoreType.DMA((CHUNKS, ROWS))]
        + [pltpu.SemaphoreType.DMA] * 2
        + [pltpu.SemaphoreType.DMA((4,))],
        compiler_params=pltpu.CompilerParams(
            collective_id=0, has_side_effects=True, vmem_limit_bytes=32 * 1024 * 1024
        ),
    )(pltpu.with_memory_space_constraint(density.reshape(16, 4, size_y, planes), pltpu.HBM))
    return coarse.reshape(size_x, size_y, planes), moments.reshape(len(SPACINGS), 4, 1, 1)


def solution(mesh):
    placed = (P("row", "col", None),)

    def program(density):
        size_x, size_y, planes = density.shape
        local = (size_x // mesh.shape["row"], size_y // mesh.shape["col"], planes)
        classes = (mesh.shape["row"], mesh.shape["col"]) == (ROWS, COLS) and local == BLOCK
        return jax.shard_map(
            per_device_classes if classes else per_device,
            mesh=mesh,
            in_specs=placed,
            out_specs=(P("row", "col", None), P()),
            check_vma=False,
        )(density)

    return program
```

```python
import jax
import jax.numpy as jnp
import ml_dtypes
import numpy as np
from jax import lax
from jax.experimental import pallas as pl
from jax.experimental.pallas import tpu as pltpu
from jax.sharding import PartitionSpec as P

SUB = 256


SPLINE_TAPS = (0.0625, 0.25, 0.375, 0.25, 0.0625)
SPACINGS = (4, 8, 16)
EPSILON = 1e-06


def padded_2(block, sides, width):
    for axis, dim in sides:
        count = lax.axis_size(axis)
        forward = [(i, i + 1) for i in range(count - 1)]
        forward.append((count - 1, 0))
        backward = [(target, source) for source, target in forward]
        low = lax.ppermute(
            lax.slice_in_dim(block, block.shape[dim] - width, None, axis=dim), axis, forward
        )
        high = lax.ppermute(lax.slice_in_dim(block, 0, width, axis=dim), axis, backward)
        block = jnp.concatenate([low, block, high], axis=dim)
    return block


def holed_pass(padded, spacing, axis_number, length_out):
    summed = SPLINE_TAPS[0] * lax.slice_in_dim(padded, 0, length_out, axis=axis_number)
    for tap_index in (1, 2, 3, 4):
        portion = lax.slice_in_dim(
            padded, tap_index * spacing, tap_index * spacing + length_out, axis=axis_number
        )
        summed = summed + SPLINE_TAPS[tap_index] * portion
    return summed


def depth_pass(values_in, spacing):
    summed = SPLINE_TAPS[2] * values_in
    for tap_index in (0, 1, 3, 4):
        summed = summed + SPLINE_TAPS[tap_index] * jnp.roll(
            values_in, -(tap_index - 2) * spacing, axis=2
        )
    return summed


def moment_planes(detail):
    square = detail * detail
    return jnp.stack(
        [
            jnp.sum(jnp.abs(detail), axis=2),
            jnp.sum(square, axis=2),
            jnp.sum(square * detail, axis=2),
            jnp.sum(square * square, axis=2),
        ]
    )


def finish_table(table, planes):
    means = table / jnp.float32(SUB * SUB * planes)
    second = means[:, 1]
    third = means[:, 2] / (second + EPSILON) ** 1.5
    fourth = means[:, 3] / (second + EPSILON) ** 2
    return jnp.stack([means[:, 0], second, third, fourth], axis=1)


def per_device(density):
    size_x, size_y, planes = density.shape
    plane_list = []
    current = density
    for spacing in SPACINGS:
        rows_padded = padded_2(current, (("row", 0),), 2 * spacing)
        along_x = holed_pass(rows_padded, spacing, 0, size_x)
        cols_padded = padded_2(along_x, (("col", 1),), 2 * spacing)
        along_y = holed_pass(cols_padded, spacing, 1, size_y)
        smoother = depth_pass(along_y, spacing)
        plane_list.append(moment_planes(current - smoother))
        current = smoother
    planes_all = jnp.stack(plane_list)
    count_x = lax.axis_size("row") * size_x // SUB
    count_y = lax.axis_size("col") * size_y // SUB
    rows_global = lax.axis_index("row") * size_x + jnp.arange(size_x, dtype=jnp.int32)
    cols_global = lax.axis_index("col") * size_y + jnp.arange(size_y, dtype=jnp.int32)
    onehot_x = (
        (rows_global // SUB)[:, None] == jnp.arange(count_x, dtype=jnp.int32)[None, :]
    ).astype(jnp.float32)
    onehot_y = (
        (cols_global // SUB)[:, None] == jnp.arange(count_y, dtype=jnp.int32)[None, :]
    ).astype(jnp.float32)
    partial_table = jnp.einsum(
        "xa,skxy,yb->skab", onehot_x, planes_all, onehot_y, precision=lax.Precision.HIGHEST
    )
    table = lax.psum(partial_table, ("row", "col"))
    return (current, finish_table(table, planes))


MESH = pl.DeviceIdType.MESH
ROWS, COLS = 4, 8
DEVICES = ROWS * COLS
BLOCK = (64, 32, 128)
CLASS_X, CLASS_Y, LANES = 64, 64, 128
CHUNKS = 2


def five_taps(low2, low1, mid, high1, high2):
    return (
        SPLINE_TAPS[0] * (low2 + high2) + SPLINE_TAPS[1] * (low1 + high1) + SPLINE_TAPS[2] * mid
    )


def roll(v, shift, axis):
    shift = shift % v.shape[axis]
    return pltpu.roll(v, shift, axis) if shift else v


KEPT = 100
SPARE = LANES - KEPT
REST = KEPT - 3 * SPARE


def range_matrices():
    cells = np.arange(32)
    columns = [np.full(32, np.sqrt(1 / 32))]
    for m in range(1, 16):
        if m % 4:
            angle = 2 * np.pi * m * cells / 32
            columns += [np.sqrt(1 / 16) * np.cos(angle), np.sqrt(1 / 16) * np.sin(angle)]
    basis = np.kron(np.stack(columns, axis=1), np.eye(4))
    whole = np.zeros((LANES, LANES))
    whole[:, :KEPT] = basis
    spare = [np.zeros((LANES, LANES)) for _ in range(3)]
    for j in range(3):
        spare[j][:, KEPT:] = basis[:, SPARE * j : SPARE * (j + 1)]
    rest = np.tile(basis[:, 3 * SPARE :], (1, LANES // REST))

    def thrice(matrix):
        high = matrix.astype(ml_dtypes.bfloat16)
        low = (matrix - high.astype(np.float64)).astype(ml_dtypes.bfloat16)
        return [high, high, low]

    parts = []
    for j in range(3):
        parts += thrice(whole) + thrice(spare[j])
    parts += thrice(rest)
    parts += thrice(whole.T)
    for j in range(3):
        parts += thrice(spare[j].T)
    parts += thrice(rest.T)
    return np.concatenate(parts, axis=0)


INTO, INTO_REST, OUT, OUT_LAST, MATRIX_ROWS = 0, 2304, 2688, 3072, 4608


def thirds(v):
    high = v.astype(jnp.bfloat16)
    low = (v - high.astype(jnp.float32)).astype(jnp.bfloat16)
    return [high, low, high]


def exchange_pair(lane, distance, first, second):
    clear = (lane & distance) == 0
    return (
        jnp.where(clear, first, roll(second, distance, 2)),
        jnp.where(clear, roll(first, -distance, 2), second),
    )


def class_kernel(
    x_hbm,
    basis_hbm,
    out_ref,
    tab_ref,
    x_ref,
    send,
    f0,
    f1,
    back,
    padded,
    taps,
    basis,
    packed,
    rests,
    sums,
    ssem,
    rsem,
    bssem,
    brsem,
    mssem,
    mrsem,
    xsem,
    basis_sem,
):
    row, col = lax.axis_index("row"), lax.axis_index("col")
    me = row * COLS + col
    col_hi, col_lo = lax.div(col, 2), lax.rem(col, 2)

    order = jnp.where(
        col_hi == 0, 30, jnp.where(col_hi == 1, 180, jnp.where(col_hi == 2, 75, 225))
    )

    planes = [lax.rem(lax.div(order, 4**step), 4) for step in range(4)]

    def each_other(visit):
        for hi in planes:

            @pl.loop(0, ROWS)
            def _(near):
                r = row + near
                r = jnp.where(r >= ROWS, r - ROWS, r)
                visit(r, 2 * hi + 1 - col_lo)

                @pl.when(r * COLS + 2 * hi + col_lo != me)
                def _():
                    visit(r, 2 * hi + col_lo)

    def place(ref, h, r, c):
        return ref.at[h, 4 * r, c]

    def load_x(rx):
        return pltpu.make_async_copy(x_hbm.at[:, rx], x_ref.at[:, rx], xsem.at[rx])

    for rx in range(4):
        load_x(rx).start()
    load_basis = pltpu.make_async_copy(basis_hbm, basis, basis_sem)
    load_basis.start()

    def times(parts, begin):
        left = jnp.concatenate(parts, axis=1)
        right = basis[begin : begin + left.shape[1], :]
        return jnp.dot(left, right, preferred_element_type=jnp.float32)

    barrier = pltpu.get_barrier_semaphore()

    each_other(
        lambda r, c: pl.semaphore_signal(
            barrier, inc=1, device_id=(r, c), device_id_type=MESH
        )
    )

    lane3 = lax.broadcasted_iota(jnp.int32, (4, 8, LANES), 2)

    def pack(h):
        @pl.loop(0, 4)
        def _(rx):
            if h == 0:
                load_x(rx).wait()
            for ry in range(4):
                v = [
                    jnp.stack([x_ref[4 * q + i, rx, pl.ds(ry, 8, stride=4), :] for i in range(4)])
                    for q in range(4)
                ]
                u0 = exchange_pair(lane3, 2, v[0], v[2])[h]
                u1 = exchange_pair(lane3, 2, v[1], v[3])[h]
                w0, w1 = exchange_pair(lane3, 1, u0, u1)
                send[h, rx * COLS + 2 * ry] = w0
                send[h, rx * COLS + 2 * ry + 1] = w1

    def forward(h, r, c, source_r, source_c):
        k = r * COLS + c
        return pltpu.make_async_remote_copy(
            src_ref=send.at[h, k],
            dst_ref=place(f0, h, source_r, source_c),
            send_sem=ssem.at[h],
            recv_sem=rsem.at[h],
            device_id=(r, c),
            device_id_type=MESH,
        )

    def send_all(h):
        each_other(lambda r, c: forward(h, r, c, row, col).start())
        f0[h, 4 * row, col] = send[h, me]

    def wait_bytes(ref, sem):
        pltpu.make_async_copy(ref, ref, sem).wait()

    others = pl.ds(0, DEVICES - 1)

    lane2 = lax.broadcasted_iota(jnp.int32, (CLASS_Y, LANES), 1)
    lane = lax.broadcasted_iota(jnp.int32, (1, LANES), 1)
    begin = REST * lax.broadcasted_iota(jnp.int32, (8, 8, LANES), 1)
    lane_8 = lax.broadcasted_iota(jnp.int32, (8, 8, LANES), 2)
    own_lanes = (lane_8 >= begin) & (lane_8 < begin + REST)

    def fill(ref, h, unit):
        for r in range(4):
            for i in range(4):
                here = ref[h, 4 * r, :, i].reshape(CLASS_Y, LANES)
                after = ref[h, 4 * ((r + 1) % 4), :, i].reshape(CLASS_Y, LANES)
                for m in (1, 2, 3):
                    reached = (i < 2 * unit, unit == 4, i >= 4 - 2 * unit)[m - 1]
                    if reached:
                        ref[h, 4 * r + m, :, i] = jnp.where(
                            (lane2 & 3) < 4 - m, roll(here, -m, 1), roll(after, 4 - m, 1)
                        ).reshape(8, 8, LANES)

    def make_taps():
        shape = (2 * LANES, LANES)
        gap = (
            lax.broadcasted_iota(jnp.int32, shape, 0) - lax.broadcasted_iota(jnp.int32, shape, 1)
        ) & (LANES - 1)
        for scale, spacing in enumerate(SPACINGS):
            matrix = jnp.zeros(shape, jnp.float32)
            for k, tap in zip(range(-2, 3), SPLINE_TAPS):
                matrix = jnp.where(gap == (k * spacing) % LANES, tap, matrix)
            taps[scale] = matrix.astype(jnp.bfloat16)

    def smooth_rows(src, dst, h, scale, r, acc):
        unit = SPACINGS[scale] // 4
        mids = []
        for i in range(4):

            def at(k):
                n = i + k * unit
                block = 4 * r + n // 4
                block = jnp.where(block < 0, block + 16, jnp.where(block >= 16, block - 16, block))
                return src[h, block, :, n % 4].reshape(CLASS_Y, LANES)

            mids.append(at(0))
            v = five_taps(at(-2), at(-1), mids[i], at(1), at(2))
            padded[i, 8:72, :] = v
            padded[i, 0:8, :] = v[56:]
            padded[i, 72:80, :] = v[:8]
        rows = []
        for i in range(4):
            rows.append(
                five_taps(*(padded[i, 8 + k * unit : 72 + k * unit, :] for k in range(-2, 3)))
            )
        v = jnp.concatenate(rows, axis=0)
        high = v.astype(jnp.bfloat16)
        low = (v - high.astype(jnp.float32)).astype(jnp.bfloat16)
        v = jnp.dot(
            jnp.concatenate([high, low], axis=1), taps[scale], preferred_element_type=jnp.float32
        )
        for i in range(4):
            smooth = v[CLASS_Y * i : CLASS_Y * (i + 1)]
            if scale < len(SPACINGS) - 1:
                dst[h, 4 * r, :, i] = smooth.reshape(8, 8, LANES)
            detail = (mids[i] - smooth).reshape(8, 8, LANES)
            square = detail * detail
            parts = (jnp.abs(detail), square, square * detail, square * square)
            acc = tuple(s + jnp.sum(p, axis=0) for s, p in zip(acc, parts))
        if scale == len(SPACINGS) - 1:
            last = v[3 * CLASS_Y :]
            for j in range(3):
                row_j = v[CLASS_Y * j : CLASS_Y * (j + 1)]
                t = times(thirds(row_j) + thirds(last), INTO + 768 * j)
                packed[h, pl.ds(8 * r, 8), j] = t.reshape(8, 8, LANES)
            t = times(thirds(last), INTO_REST).reshape(8, 8, LANES)
            t = jnp.sum(jnp.where(own_lanes, t, 0.0), axis=1)
            for c in range(COLS):
                rests[8 * r + c, h] = t[c : c + 1]
        return acc

    def backward(h, r, c, source_r, source_c):
        source = source_r * COLS + source_c
        return pltpu.make_async_remote_copy(
            src_ref=packed.at[h, r * COLS + c],
            dst_ref=back.at[h, source],
            send_sem=bssem.at[h],
            recv_sem=brsem.at[h, source_r],
            device_id=(r, c),
            device_id_type=MESH,
        )

    def scales(h, accs):
        fields = (f0, f1, f0, f1)
        results = []
        for scale, spacing in enumerate(SPACINGS):
            src, dst = fields[scale], fields[scale + 1]
            fill(src, h, spacing // 4)

            acc = accs[scale]
            for near in range(4):
                r = row + near
                r = jnp.where(r >= ROWS, r - ROWS, r)
                acc = smooth_rows(src, dst, h, scale, r, acc)
                if scale == len(SPACINGS) - 1:
                    for hi in planes:
                        for c in (2 * hi + 1 - col_lo, 2 * hi + col_lo):

                            @pl.when(r * COLS + c != me)
                            def _():
                                backward(h, r, c, row, col).start()

            results.append(acc)
        back[h, me] = packed[h, me]
        return results

    make_taps()
    pack(0)
    pl.semaphore_wait(barrier, DEVICES - 1)
    send_all(0)
    pack(1)
    send_all(1)
    accs = [(jnp.zeros((8, LANES), jnp.float32),) * 4] * len(SPACINGS)

    def chunk(h, accs):
        wait_bytes(send.at[h, others], rsem.at[h])
        return scales(h, accs)

    load_basis.wait()
    accs = lax.fori_loop(0, CHUNKS, chunk, accs)

    total = jnp.zeros((1, LANES), jnp.float32)
    for scale, acc in enumerate(accs):
        for moment, s in enumerate(acc):
            value = jnp.sum(jnp.sum(s, axis=0, keepdims=True), axis=1, keepdims=True)
            total = total + jnp.where(lane == 4 * scale + moment, value, 0.0)
    for k in range(DEVICES):
        rests[k, 2] = total
    sums[me] = rests[me]

    def share(r, c, source):
        return pltpu.make_async_remote_copy(
            src_ref=rests.at[r * COLS + c],
            dst_ref=sums.at[source],
            send_sem=mssem,
            recv_sem=mrsem,
            device_id=(r, c),
            device_id_type=MESH,
        )

    each_other(lambda r, c: share(r, c, me).start())
    wait_bytes(sums.at[others], mrsem)

    @pl.loop(0, 4)
    def _(j):
        rx = lax.rem(row + 4 - j, 4)
        for h in range(CHUNKS):

            @pl.when(rx == row)
            def _():
                wait_bytes(packed.at[h, pl.ds(0, COLS - 1)], brsem.at[h, rx])

            @pl.when(rx != row)
            def _():
                wait_bytes(packed.at[h, pl.ds(0, COLS)], brsem.at[h, rx])

        rows = []
        for h in range(CHUNKS):
            parts = [back[h, pl.ds(8 * rx, 8), k].reshape(CLASS_Y, LANES) for k in range(3)]
            rest = jnp.stack([jnp.broadcast_to(sums[8 * rx + c, h], (8, LANES)) for c in range(COLS)])
            rest = jnp.where(own_lanes, rest, 0.0).reshape(CLASS_Y, LANES)
            thirds_of = [thirds(v) for v in parts + [rest]]
            rows.append([times(t, OUT) for t in thirds_of[:3]] + [times(sum(thirds_of, []), OUT_LAST)])
        for ry in range(4):
            u = []
            for h in range(CHUNKS):
                w = [
                    jnp.stack([v[8 * c : 8 * c + 8] for v in rows[h]])
                    for c in (2 * ry, 2 * ry + 1)
                ]
                u.append(exchange_pair(lane3, 1, w[0], w[1]))
            for q in range(2):
                for low, v in enumerate(exchange_pair(lane3, 2, u[0][q], u[1][q])):
                    for i in range(4):
                        out_ref[4 * (q + 2 * low) + i, rx, pl.ds(ry, 8, stride=4), :] = v[i]

    wait_bytes(sums.at[others], mssem)
    for h in range(CHUNKS):
        wait_bytes(send.at[h, others], ssem.at[h])
        wait_bytes(packed.at[h, others], bssem.at[h])

    means = sum(sums[k, 2] for k in range(DEVICES)) / jnp.float32(SUB * SUB * LANES)
    moment = lane & 3
    second = jnp.where(moment == 2, roll(means, 1, 1), roll(means, 2, 1)) + EPSILON
    power = second * jnp.where(moment == 2, jnp.sqrt(second), second)
    final = jnp.where(moment < 2, means, means / power)
    for scale in range(len(SPACINGS)):
        tab_ref[scale] = final[:, 4 * scale : 4 * scale + 4]


def per_device_classes(density):
    size_x, size_y, planes = density.shape
    dma = pltpu.SemaphoreType.DMA((CHUNKS,))
    block = pltpu.VMEM((CHUNKS, DEVICES, 4, 8, LANES), jnp.float32)
    part = pltpu.VMEM((CHUNKS, DEVICES, 3, 8, LANES), jnp.float32)
    rests = pltpu.VMEM((DEVICES, 3, 1, LANES), jnp.float32)
    field = pltpu.VMEM((CHUNKS, CLASS_X // 4, CLASS_Y // 8, 4, 8, LANES), jnp.float32)
    coarse, moments = pl.pallas_call(
        class_kernel,
        out_shape=(
            jax.ShapeDtypeStruct((16, 4, size_y, planes), jnp.float32),
            jax.ShapeDtypeStruct((len(SPACINGS), 1, 4), jnp.float32),
        ),
        in_specs=[pl.BlockSpec(memory_space=pltpu.HBM)] * 2,
        out_specs=(pl.BlockSpec(memory_space=pltpu.VMEM),) * 2,
        scratch_shapes=[
            pltpu.VMEM((16, 4, size_y, planes), jnp.float32),
            block,
            field,
            field,
            part,
            pltpu.VMEM((4, CLASS_Y + 16, LANES), jnp.float32),
            pltpu.VMEM((len(SPACINGS), 2 * LANES, LANES), jnp.bfloat16),
            pltpu.VMEM((MATRIX_ROWS, LANES), jnp.bfloat16),
            part,
            rests,
            rests,
        ]
        + [dma] * 3
        + [pltpu.SemaphoreType.DMA((CHUNKS, ROWS))]
        + [pltpu.SemaphoreType.DMA] * 2
        + [pltpu.SemaphoreType.DMA((4,)), pltpu.SemaphoreType.DMA],
        compiler_params=pltpu.CompilerParams(
            collective_id=0, has_side_effects=True, vmem_limit_bytes=32 * 1024 * 1024
        ),
    )(
        pltpu.with_memory_space_constraint(density.reshape(16, 4, size_y, planes), pltpu.HBM),
        pltpu.with_memory_space_constraint(jnp.asarray(range_matrices()), pltpu.HBM),
    )
    return coarse.reshape(size_x, size_y, planes), moments.reshape(len(SPACINGS), 4, 1, 1)


def solution(mesh):
    placed = (P("row", "col", None),)

    def program(density):
        size_x, size_y, planes = density.shape
        local = (size_x // mesh.shape["row"], size_y // mesh.shape["col"], planes)
        classes = (mesh.shape["row"], mesh.shape["col"]) == (ROWS, COLS) and local == BLOCK
        return jax.shard_map(
            per_device_classes if classes else per_device,
            mesh=mesh,
            in_specs=placed,
            out_specs=(P("row", "col", None), P()),
            check_vma=False,
        )(density)

    return program
```

```python
import jax
import jax.numpy as jnp
import ml_dtypes
import numpy as np
from jax import lax
from jax.experimental import pallas as pl
from jax.experimental.pallas import tpu as pltpu
from jax.sharding import PartitionSpec as P

SUB = 256


SPLINE_TAPS = (0.0625, 0.25, 0.375, 0.25, 0.0625)
SPACINGS = (4, 8, 16)
EPSILON = 1e-06


def padded_2(block, sides, width):
    for axis, dim in sides:
        count = lax.axis_size(axis)
        forward = [(i, i + 1) for i in range(count - 1)]
        forward.append((count - 1, 0))
        backward = [(target, source) for source, target in forward]
        low = lax.ppermute(
            lax.slice_in_dim(block, block.shape[dim] - width, None, axis=dim), axis, forward
        )
        high = lax.ppermute(lax.slice_in_dim(block, 0, width, axis=dim), axis, backward)
        block = jnp.concatenate([low, block, high], axis=dim)
    return block


def holed_pass(padded, spacing, axis_number, length_out):
    summed = SPLINE_TAPS[0] * lax.slice_in_dim(padded, 0, length_out, axis=axis_number)
    for tap_index in (1, 2, 3, 4):
        portion = lax.slice_in_dim(
            padded, tap_index * spacing, tap_index * spacing + length_out, axis=axis_number
        )
        summed = summed + SPLINE_TAPS[tap_index] * portion
    return summed


def depth_pass(values_in, spacing):
    summed = SPLINE_TAPS[2] * values_in
    for tap_index in (0, 1, 3, 4):
        summed = summed + SPLINE_TAPS[tap_index] * jnp.roll(
            values_in, -(tap_index - 2) * spacing, axis=2
        )
    return summed


def moment_planes(detail):
    square = detail * detail
    return jnp.stack(
        [
            jnp.sum(jnp.abs(detail), axis=2),
            jnp.sum(square, axis=2),
            jnp.sum(square * detail, axis=2),
            jnp.sum(square * square, axis=2),
        ]
    )


def finish_table(table, planes):
    means = table / jnp.float32(SUB * SUB * planes)
    second = means[:, 1]
    third = means[:, 2] / (second + EPSILON) ** 1.5
    fourth = means[:, 3] / (second + EPSILON) ** 2
    return jnp.stack([means[:, 0], second, third, fourth], axis=1)


def per_device(density):
    size_x, size_y, planes = density.shape
    plane_list = []
    current = density
    for spacing in SPACINGS:
        rows_padded = padded_2(current, (("row", 0),), 2 * spacing)
        along_x = holed_pass(rows_padded, spacing, 0, size_x)
        cols_padded = padded_2(along_x, (("col", 1),), 2 * spacing)
        along_y = holed_pass(cols_padded, spacing, 1, size_y)
        smoother = depth_pass(along_y, spacing)
        plane_list.append(moment_planes(current - smoother))
        current = smoother
    planes_all = jnp.stack(plane_list)
    count_x = lax.axis_size("row") * size_x // SUB
    count_y = lax.axis_size("col") * size_y // SUB
    rows_global = lax.axis_index("row") * size_x + jnp.arange(size_x, dtype=jnp.int32)
    cols_global = lax.axis_index("col") * size_y + jnp.arange(size_y, dtype=jnp.int32)
    onehot_x = (
        (rows_global // SUB)[:, None] == jnp.arange(count_x, dtype=jnp.int32)[None, :]
    ).astype(jnp.float32)
    onehot_y = (
        (cols_global // SUB)[:, None] == jnp.arange(count_y, dtype=jnp.int32)[None, :]
    ).astype(jnp.float32)
    partial_table = jnp.einsum(
        "xa,skxy,yb->skab", onehot_x, planes_all, onehot_y, precision=lax.Precision.HIGHEST
    )
    table = lax.psum(partial_table, ("row", "col"))
    return (current, finish_table(table, planes))


MESH = pl.DeviceIdType.MESH
ROWS, COLS = 4, 8
DEVICES = ROWS * COLS
BLOCK = (64, 32, 128)
CLASS_X, CLASS_Y, LANES = 64, 64, 128
CHUNKS = 2


def five_taps(low2, low1, mid, high1, high2):
    return (
        SPLINE_TAPS[0] * (low2 + high2) + SPLINE_TAPS[1] * (low1 + high1) + SPLINE_TAPS[2] * mid
    )


def roll(v, shift, axis):
    shift = shift % v.shape[axis]
    return pltpu.roll(v, shift, axis) if shift else v


KEPT = 100
SPARE = LANES - KEPT
REST = KEPT - 3 * SPARE


def range_matrices():
    cells = np.arange(32)
    columns = [np.full(32, np.sqrt(1 / 32))]
    for m in range(1, 16):
        if m % 4:
            angle = 2 * np.pi * m * cells / 32
            columns += [np.sqrt(1 / 16) * np.cos(angle), np.sqrt(1 / 16) * np.sin(angle)]
    basis = np.kron(np.stack(columns, axis=1), np.eye(4))
    whole = np.zeros((LANES, LANES))
    whole[:, :KEPT] = basis
    spare = [np.zeros((LANES, LANES)) for _ in range(3)]
    for j in range(3):
        spare[j][:, KEPT:] = basis[:, SPARE * j : SPARE * (j + 1)]
    rest = np.tile(basis[:, 3 * SPARE :], (1, LANES // REST))

    def thrice(matrix):
        high = matrix.astype(ml_dtypes.bfloat16)
        low = (matrix - high.astype(np.float64)).astype(ml_dtypes.bfloat16)
        return [high, high, low]

    parts = []
    for j in range(3):
        parts += thrice(whole) + thrice(spare[j])
    parts += thrice(rest)
    parts += thrice(whole.T)
    for j in range(3):
        parts += thrice(spare[j].T)
    parts += thrice(rest.T)
    return np.concatenate(parts, axis=0)


INTO, INTO_REST, OUT, OUT_LAST, MATRIX_ROWS = 0, 2304, 2688, 3072, 4608


def thirds(v):
    high = v.astype(jnp.bfloat16)
    low = (v - high.astype(jnp.float32)).astype(jnp.bfloat16)
    return [high, low, high]


def exchange_pair(lane, distance, first, second):
    clear = (lane & distance) == 0
    return (
        jnp.where(clear, first, roll(second, distance, 2)),
        jnp.where(clear, roll(first, -distance, 2), second),
    )


def class_kernel(
    x_hbm,
    basis_hbm,
    out_ref,
    tab_ref,
    x_ref,
    send,
    f0,
    f1,
    back,
    padded,
    taps,
    basis,
    packed,
    rests,
    sums,
    ssem,
    rsem,
    bssem,
    brsem,
    mssem,
    mrsem,
    xsem,
    basis_sem,
):
    row, col = lax.axis_index("row"), lax.axis_index("col")
    me = row * COLS + col
    col_hi, col_lo = lax.div(col, 2), lax.rem(col, 2)

    order = jnp.where(
        col_hi == 0, 30, jnp.where(col_hi == 1, 180, jnp.where(col_hi == 2, 75, 225))
    )

    planes = [lax.rem(lax.div(order, 4**step), 4) for step in range(4)]

    def each_other(visit):
        for hi in planes:

            @pl.loop(0, ROWS)
            def _(near):
                r = row + near
                r = jnp.where(r >= ROWS, r - ROWS, r)
                visit(r, 2 * hi + 1 - col_lo)

                @pl.when(r * COLS + 2 * hi + col_lo != me)
                def _():
                    visit(r, 2 * hi + col_lo)

    def place(ref, h, r, c):
        return ref.at[h, 4 * r, c]

    def load_x(rx):
        return pltpu.make_async_copy(x_hbm.at[:, rx], x_ref.at[:, rx], xsem.at[rx])

    for rx in range(4):
        load_x(rx).start()
    load_basis = pltpu.make_async_copy(basis_hbm, basis, basis_sem)
    load_basis.start()

    def times(parts, begin):
        left = jnp.concatenate(parts, axis=1)
        right = basis[begin : begin + left.shape[1], :]
        return jnp.dot(left, right, preferred_element_type=jnp.float32)

    barrier = pltpu.get_barrier_semaphore()

    each_other(
        lambda r, c: pl.semaphore_signal(
            barrier, inc=1, device_id=(r, c), device_id_type=MESH
        )
    )

    lane3 = lax.broadcasted_iota(jnp.int32, (4, 8, LANES), 2)

    def pack(h):
        @pl.loop(0, 4)
        def _(rx):
            if h == 0:
                load_x(rx).wait()
            for ry in range(4):
                v = [
                    jnp.stack([x_ref[4 * q + i, rx, pl.ds(ry, 8, stride=4), :] for i in range(4)])
                    for q in range(4)
                ]
                u0 = exchange_pair(lane3, 2, v[0], v[2])[h]
                u1 = exchange_pair(lane3, 2, v[1], v[3])[h]
                w0, w1 = exchange_pair(lane3, 1, u0, u1)
                send[h, rx * COLS + 2 * ry] = w0
                send[h, rx * COLS + 2 * ry + 1] = w1

    def forward(h, r, c, source_r, source_c):
        k = r * COLS + c
        return pltpu.make_async_remote_copy(
            src_ref=send.at[h, k],
            dst_ref=place(f0, h, source_r, source_c),
            send_sem=ssem.at[h],
            recv_sem=rsem.at[h],
            device_id=(r, c),
            device_id_type=MESH,
        )

    def send_all(h):
        each_other(lambda r, c: forward(h, r, c, row, col).start())
        f0[h, 4 * row, col] = send[h, me]

    def wait_bytes(ref, sem):
        pltpu.make_async_copy(ref, ref, sem).wait()

    others = pl.ds(0, DEVICES - 1)

    lane2 = lax.broadcasted_iota(jnp.int32, (CLASS_Y, LANES), 1)
    lane = lax.broadcasted_iota(jnp.int32, (1, LANES), 1)
    begin = REST * lax.broadcasted_iota(jnp.int32, (8, 8, LANES), 1)
    lane_8 = lax.broadcasted_iota(jnp.int32, (8, 8, LANES), 2)
    own_lanes = (lane_8 >= begin) & (lane_8 < begin + REST)

    def fill(ref, h, unit):
        for r in range(4):
            for i in range(4):
                here = ref[h, 4 * r, :, i].reshape(CLASS_Y, LANES)
                after = ref[h, 4 * ((r + 1) % 4), :, i].reshape(CLASS_Y, LANES)
                for m in (1, 2, 3):
                    reached = (i < 2 * unit, unit == 4, i >= 4 - 2 * unit)[m - 1]
                    if reached:
                        ref[h, 4 * r + m, :, i] = jnp.where(
                            (lane2 & 3) < 4 - m, roll(here, -m, 1), roll(after, 4 - m, 1)
                        ).reshape(8, 8, LANES)

    def make_taps():
        shape = (2 * LANES, LANES)
        gap = (
            lax.broadcasted_iota(jnp.int32, shape, 0) - lax.broadcasted_iota(jnp.int32, shape, 1)
        ) & (LANES - 1)
        for scale, spacing in enumerate(SPACINGS):
            matrix = jnp.zeros(shape, jnp.float32)
            for k, tap in zip(range(-2, 3), SPLINE_TAPS):
                matrix = jnp.where(gap == (k * spacing) % LANES, tap, matrix)
            taps[scale] = matrix.astype(jnp.bfloat16)

    def smooth_rows(src, dst, h, scale, r, acc):
        unit = SPACINGS[scale] // 4
        mids = []
        for i in range(4):

            def at(k):
                n = i + k * unit
                block = 4 * r + n // 4
                block = jnp.where(block < 0, block + 16, jnp.where(block >= 16, block - 16, block))
                return src[h, block, :, n % 4].reshape(CLASS_Y, LANES)

            mids.append(at(0))
            v = five_taps(at(-2), at(-1), mids[i], at(1), at(2))
            padded[i, 8:72, :] = v
            padded[i, 0:8, :] = v[56:]
            padded[i, 72:80, :] = v[:8]
        rows = []
        for i in range(4):
            rows.append(
                five_taps(*(padded[i, 8 + k * unit : 72 + k * unit, :] for k in range(-2, 3)))
            )
        v = jnp.concatenate(rows, axis=0)
        high = v.astype(jnp.bfloat16)
        low = (v - high.astype(jnp.float32)).astype(jnp.bfloat16)
        v = jnp.dot(
            jnp.concatenate([high, low], axis=1), taps[scale], preferred_element_type=jnp.float32
        )
        for i in range(4):
            smooth = v[CLASS_Y * i : CLASS_Y * (i + 1)]
            if scale < len(SPACINGS) - 1:
                dst[h, 4 * r, :, i] = smooth.reshape(8, 8, LANES)
            detail = (mids[i] - smooth).reshape(8, 8, LANES)
            square = detail * detail
            parts = (jnp.abs(detail), square, square * detail, square * square)
            acc = tuple(s + jnp.sum(p, axis=0) for s, p in zip(acc, parts))
        if scale == len(SPACINGS) - 1:
            last = v[3 * CLASS_Y :]
            for j in range(3):
                row_j = v[CLASS_Y * j : CLASS_Y * (j + 1)]
                t = times(thirds(row_j) + thirds(last), INTO + 768 * j)
                packed[h, pl.ds(8 * r, 8), j] = t.reshape(8, 8, LANES)
            t = times(thirds(last), INTO_REST).reshape(8, 8, LANES)
            t = jnp.sum(jnp.where(own_lanes, t, 0.0), axis=1)
            for c in range(COLS):
                rests[8 * r + c, h] = t[c : c + 1]
        return acc

    def backward(h, r, c, source_r, source_c):
        source = source_r * COLS + source_c
        return pltpu.make_async_remote_copy(
            src_ref=packed.at[h, r * COLS + c],
            dst_ref=back.at[h, source],
            send_sem=bssem.at[h],
            recv_sem=brsem.at[h, source_r],
            device_id=(r, c),
            device_id_type=MESH,
        )

    def scales(h, accs):
        fields = (f0, f1, f0, f1)
        results = []
        for scale, spacing in enumerate(SPACINGS):
            src, dst = fields[scale], fields[scale + 1]
            fill(src, h, spacing // 4)

            acc = accs[scale]
            for near in range(4):
                r = row + near
                r = jnp.where(r >= ROWS, r - ROWS, r)
                acc = smooth_rows(src, dst, h, scale, r, acc)
                if scale == len(SPACINGS) - 1:
                    for hi in planes:
                        for c in (2 * hi + 1 - col_lo, 2 * hi + col_lo):

                            @pl.when(r * COLS + c != me)
                            def _():
                                backward(h, r, c, row, col).start()

            results.append(acc)
        back[h, me] = packed[h, me]
        return results

    make_taps()
    pack(0)
    pl.semaphore_wait(barrier, DEVICES - 1)
    send_all(0)
    pack(1)
    send_all(1)
    accs = [(jnp.zeros((8, LANES), jnp.float32),) * 4] * len(SPACINGS)

    def chunk(h, accs):
        wait_bytes(send.at[h, others], rsem.at[h])
        return scales(h, accs)

    load_basis.wait()
    accs = lax.fori_loop(0, CHUNKS, chunk, accs)

    total = jnp.zeros((1, LANES), jnp.float32)
    for scale, acc in enumerate(accs):
        for moment, s in enumerate(acc):
            value = jnp.sum(jnp.sum(s, axis=0, keepdims=True), axis=1, keepdims=True)
            total = total + jnp.where(lane == 4 * scale + moment, value, 0.0)
    for k in range(DEVICES):
        rests[k, 2] = total
    sums[me] = rests[me]

    def share(r, c, source):
        return pltpu.make_async_remote_copy(
            src_ref=rests.at[r * COLS + c],
            dst_ref=sums.at[source],
            send_sem=mssem,
            recv_sem=mrsem,
            device_id=(r, c),
            device_id_type=MESH,
        )

    each_other(lambda r, c: share(r, c, me).start())

    def wait_back(h, rx):
        @pl.when(rx == row)
        def _():
            wait_bytes(packed.at[h, pl.ds(0, COLS - 1)], brsem.at[h, rx])

        @pl.when(rx != row)
        def _():
            wait_bytes(packed.at[h, pl.ds(0, COLS)], brsem.at[h, rx])

    def back_thirds(h, rx):
        return [thirds(back[h, pl.ds(8 * rx, 8), k].reshape(CLASS_Y, LANES)) for k in range(3)]

    @pl.loop(0, 4)
    def _(j):
        rx = row - j
        rx = jnp.where(rx < 0, rx + ROWS, rx)
        wait_back(0, rx)
        parts = back_thirds(0, rx)
        for k in range(3):
            f0[0, rx, :, k] = times(parts[k], OUT).reshape(8, 8, LANES)
        f0[0, rx, :, 3] = times(sum(parts, []), OUT_LAST).reshape(8, 8, LANES)

    wait_bytes(sums.at[others], mrsem)

    @pl.loop(0, 4)
    def _(j):
        rx = lax.rem(row + 4 - j, 4)
        wait_back(1, rx)
        rows = []
        for h in range(CHUNKS):
            rest = jnp.stack([jnp.broadcast_to(sums[8 * rx + c, h], (8, LANES)) for c in range(COLS)])
            rest = thirds(jnp.where(own_lanes, rest, 0.0).reshape(CLASS_Y, LANES))
            if h == 0:
                lines = [f0[0, rx, :, k].reshape(CLASS_Y, LANES) for k in range(4)]
                lines[3] = lines[3] + times(rest, OUT_LAST + 1152)
            else:
                parts = back_thirds(h, rx)
                lines = [times(t, OUT) for t in parts] + [times(sum(parts, []) + rest, OUT_LAST)]
            rows.append(lines)
        for ry in range(4):
            u = []
            for h in range(CHUNKS):
                w = [
                    jnp.stack([v[8 * c : 8 * c + 8] for v in rows[h]])
                    for c in (2 * ry, 2 * ry + 1)
                ]
                u.append(exchange_pair(lane3, 1, w[0], w[1]))
            for q in range(2):
                for low, v in enumerate(exchange_pair(lane3, 2, u[0][q], u[1][q])):
                    for i in range(4):
                        out_ref[4 * (q + 2 * low) + i, rx, pl.ds(ry, 8, stride=4), :] = v[i]

    wait_bytes(sums.at[others], mssem)
    for h in range(CHUNKS):
        wait_bytes(send.at[h, others], ssem.at[h])
        wait_bytes(packed.at[h, others], bssem.at[h])

    means = sum(sums[k, 2] for k in range(DEVICES)) / jnp.float32(SUB * SUB * LANES)
    moment = lane & 3
    second = jnp.where(moment == 2, roll(means, 1, 1), roll(means, 2, 1)) + EPSILON
    power = second * jnp.where(moment == 2, jnp.sqrt(second), second)
    final = jnp.where(moment < 2, means, means / power)
    for scale in range(len(SPACINGS)):
        tab_ref[scale] = final[:, 4 * scale : 4 * scale + 4]


def per_device_classes(density):
    size_x, size_y, planes = density.shape
    dma = pltpu.SemaphoreType.DMA((CHUNKS,))
    block = pltpu.VMEM((CHUNKS, DEVICES, 4, 8, LANES), jnp.float32)
    part = pltpu.VMEM((CHUNKS, DEVICES, 3, 8, LANES), jnp.float32)
    rests = pltpu.VMEM((DEVICES, 3, 1, LANES), jnp.float32)
    field = pltpu.VMEM((CHUNKS, CLASS_X // 4, CLASS_Y // 8, 4, 8, LANES), jnp.float32)
    coarse, moments = pl.pallas_call(
        class_kernel,
        out_shape=(
            jax.ShapeDtypeStruct((16, 4, size_y, planes), jnp.float32),
            jax.ShapeDtypeStruct((len(SPACINGS), 1, 4), jnp.float32),
        ),
        in_specs=[pl.BlockSpec(memory_space=pltpu.HBM)] * 2,
        out_specs=(pl.BlockSpec(memory_space=pltpu.VMEM),) * 2,
        scratch_shapes=[
            pltpu.VMEM((16, 4, size_y, planes), jnp.float32),
            block,
            field,
            field,
            part,
            pltpu.VMEM((4, CLASS_Y + 16, LANES), jnp.float32),
            pltpu.VMEM((len(SPACINGS), 2 * LANES, LANES), jnp.bfloat16),
            pltpu.VMEM((MATRIX_ROWS, LANES), jnp.bfloat16),
            part,
            rests,
            rests,
        ]
        + [dma] * 3
        + [pltpu.SemaphoreType.DMA((CHUNKS, ROWS))]
        + [pltpu.SemaphoreType.DMA] * 2
        + [pltpu.SemaphoreType.DMA((4,)), pltpu.SemaphoreType.DMA],
        compiler_params=pltpu.CompilerParams(
            collective_id=0, has_side_effects=True, vmem_limit_bytes=32 * 1024 * 1024
        ),
    )(
        pltpu.with_memory_space_constraint(density.reshape(16, 4, size_y, planes), pltpu.HBM),
        pltpu.with_memory_space_constraint(jnp.asarray(range_matrices()), pltpu.HBM),
    )
    return coarse.reshape(size_x, size_y, planes), moments.reshape(len(SPACINGS), 4, 1, 1)


def solution(mesh):
    placed = (P("row", "col", None),)

    def program(density):
        size_x, size_y, planes = density.shape
        local = (size_x // mesh.shape["row"], size_y // mesh.shape["col"], planes)
        classes = (mesh.shape["row"], mesh.shape["col"]) == (ROWS, COLS) and local == BLOCK
        return jax.shard_map(
            per_device_classes if classes else per_device,
            mesh=mesh,
            in_specs=placed,
            out_specs=(P("row", "col", None), P()),
            check_vma=False,
        )(density)

    return program
```

```python
import jax
import jax.numpy as jnp
import ml_dtypes
import numpy as np
from jax import lax
from jax.experimental import pallas as pl
from jax.experimental.pallas import tpu as pltpu
from jax.sharding import PartitionSpec as P

SUB = 256


SPLINE_TAPS = (0.0625, 0.25, 0.375, 0.25, 0.0625)
SPACINGS = (4, 8, 16)
EPSILON = 1e-06


def padded_2(block, sides, width):
    for axis, dim in sides:
        count = lax.axis_size(axis)
        forward = [(i, i + 1) for i in range(count - 1)]
        forward.append((count - 1, 0))
        backward = [(target, source) for source, target in forward]
        low = lax.ppermute(
            lax.slice_in_dim(block, block.shape[dim] - width, None, axis=dim), axis, forward
        )
        high = lax.ppermute(lax.slice_in_dim(block, 0, width, axis=dim), axis, backward)
        block = jnp.concatenate([low, block, high], axis=dim)
    return block


def holed_pass(padded, spacing, axis_number, length_out):
    summed = SPLINE_TAPS[0] * lax.slice_in_dim(padded, 0, length_out, axis=axis_number)
    for tap_index in (1, 2, 3, 4):
        portion = lax.slice_in_dim(
            padded, tap_index * spacing, tap_index * spacing + length_out, axis=axis_number
        )
        summed = summed + SPLINE_TAPS[tap_index] * portion
    return summed


def depth_pass(values_in, spacing):
    summed = SPLINE_TAPS[2] * values_in
    for tap_index in (0, 1, 3, 4):
        summed = summed + SPLINE_TAPS[tap_index] * jnp.roll(
            values_in, -(tap_index - 2) * spacing, axis=2
        )
    return summed


def moment_planes(detail):
    square = detail * detail
    return jnp.stack(
        [
            jnp.sum(jnp.abs(detail), axis=2),
            jnp.sum(square, axis=2),
            jnp.sum(square * detail, axis=2),
            jnp.sum(square * square, axis=2),
        ]
    )


def finish_table(table, planes):
    means = table / jnp.float32(SUB * SUB * planes)
    second = means[:, 1]
    third = means[:, 2] / (second + EPSILON) ** 1.5
    fourth = means[:, 3] / (second + EPSILON) ** 2
    return jnp.stack([means[:, 0], second, third, fourth], axis=1)


def per_device(density):
    size_x, size_y, planes = density.shape
    plane_list = []
    current = density
    for spacing in SPACINGS:
        rows_padded = padded_2(current, (("row", 0),), 2 * spacing)
        along_x = holed_pass(rows_padded, spacing, 0, size_x)
        cols_padded = padded_2(along_x, (("col", 1),), 2 * spacing)
        along_y = holed_pass(cols_padded, spacing, 1, size_y)
        smoother = depth_pass(along_y, spacing)
        plane_list.append(moment_planes(current - smoother))
        current = smoother
    planes_all = jnp.stack(plane_list)
    count_x = lax.axis_size("row") * size_x // SUB
    count_y = lax.axis_size("col") * size_y // SUB
    rows_global = lax.axis_index("row") * size_x + jnp.arange(size_x, dtype=jnp.int32)
    cols_global = lax.axis_index("col") * size_y + jnp.arange(size_y, dtype=jnp.int32)
    onehot_x = (
        (rows_global // SUB)[:, None] == jnp.arange(count_x, dtype=jnp.int32)[None, :]
    ).astype(jnp.float32)
    onehot_y = (
        (cols_global // SUB)[:, None] == jnp.arange(count_y, dtype=jnp.int32)[None, :]
    ).astype(jnp.float32)
    partial_table = jnp.einsum(
        "xa,skxy,yb->skab", onehot_x, planes_all, onehot_y, precision=lax.Precision.HIGHEST
    )
    table = lax.psum(partial_table, ("row", "col"))
    return (current, finish_table(table, planes))


MESH = pl.DeviceIdType.MESH
ROWS, COLS = 4, 8
DEVICES = ROWS * COLS
BLOCK = (64, 32, 128)
CLASS_X, CLASS_Y, LANES = 64, 64, 128
CHUNKS = 2


def five_taps(low2, low1, mid, high1, high2):
    return (
        SPLINE_TAPS[0] * (low2 + high2) + SPLINE_TAPS[1] * (low1 + high1) + SPLINE_TAPS[2] * mid
    )


def roll(v, shift, axis):
    shift = shift % v.shape[axis]
    return pltpu.roll(v, shift, axis) if shift else v


KEPT = 100
SPARE = LANES - KEPT
REST = KEPT - 3 * SPARE


def range_matrices():
    cells = np.arange(32)
    columns = [np.full(32, np.sqrt(1 / 32))]
    for m in range(1, 16):
        if m % 4:
            angle = 2 * np.pi * m * cells / 32
            columns += [np.sqrt(1 / 16) * np.cos(angle), np.sqrt(1 / 16) * np.sin(angle)]
    basis = np.kron(np.stack(columns, axis=1), np.eye(4))
    whole = np.zeros((LANES, LANES))
    whole[:, :KEPT] = basis
    spare = [np.zeros((LANES, LANES)) for _ in range(3)]
    for j in range(3):
        spare[j][:, KEPT:] = basis[:, SPARE * j : SPARE * (j + 1)]
    rest = np.tile(basis[:, 3 * SPARE :], (1, LANES // REST))

    def thrice(matrix):
        high = matrix.astype(ml_dtypes.bfloat16)
        low = (matrix - high.astype(np.float64)).astype(ml_dtypes.bfloat16)
        return [high, high, low]

    parts = []
    for j in range(3):
        parts += thrice(whole) + thrice(spare[j])
    parts += thrice(rest)
    parts += thrice(whole.T)
    for j in range(3):
        parts += thrice(spare[j].T)
    parts += thrice(rest.T)
    return np.concatenate(parts, axis=0)


INTO, INTO_REST, OUT, OUT_LAST, MATRIX_ROWS = 0, 2304, 2688, 3072, 4608


def thirds(v):
    high = v.astype(jnp.bfloat16)
    low = (v - high.astype(jnp.float32)).astype(jnp.bfloat16)
    return [high, low, high]


def exchange_pair(lane, distance, first, second):
    clear = (lane & distance) == 0
    return (
        jnp.where(clear, first, roll(second, distance, 2)),
        jnp.where(clear, roll(first, -distance, 2), second),
    )


def class_kernel(
    x_hbm,
    basis_hbm,
    out_ref,
    tab_ref,
    x_ref,
    send,
    f0,
    f1,
    back,
    padded,
    taps,
    basis,
    packed,
    rests,
    sums,
    ssem,
    rsem,
    bssem,
    brsem,
    mssem,
    mrsem,
    xsem,
    basis_sem,
):
    row, col = lax.axis_index("row"), lax.axis_index("col")
    me = row * COLS + col
    col_hi, col_lo = lax.div(col, 2), lax.rem(col, 2)

    order = jnp.where(
        col_hi == 0, 30, jnp.where(col_hi == 1, 180, jnp.where(col_hi == 2, 75, 225))
    )

    planes = [lax.rem(lax.div(order, 4**step), 4) for step in range(4)]

    def each_other(visit):
        @pl.loop(0, ROWS)
        def _(near):
            r = row + near
            r = jnp.where(r >= ROWS, r - ROWS, r)
            for hi in planes:
                visit(r, 2 * hi + 1 - col_lo)
            for hi in planes:

                @pl.when(r * COLS + 2 * hi + col_lo != me)
                def _():
                    visit(r, 2 * hi + col_lo)

    def place(ref, h, r, c):
        return ref.at[h, 4 * r, c]

    def load_x(rx):
        return pltpu.make_async_copy(x_hbm.at[:, rx], x_ref.at[:, rx], xsem.at[rx])

    for rx in range(4):
        load_x(rx).start()
    load_basis = pltpu.make_async_copy(basis_hbm, basis, basis_sem)
    load_basis.start()

    def times(parts, begin):
        left = jnp.concatenate(parts, axis=1)
        right = basis[begin : begin + left.shape[1], :]
        return jnp.dot(left, right, preferred_element_type=jnp.float32)

    barrier = pltpu.get_barrier_semaphore()

    each_other(
        lambda r, c: pl.semaphore_signal(
            barrier, inc=1, device_id=(r, c), device_id_type=MESH
        )
    )

    lane3 = lax.broadcasted_iota(jnp.int32, (4, 8, LANES), 2)

    def pack(h):
        @pl.loop(0, 4)
        def _(rx):
            if h == 0:
                load_x(rx).wait()
            for ry in range(4):
                v = [
                    jnp.stack([x_ref[4 * q + i, rx, pl.ds(ry, 8, stride=4), :] for i in range(4)])
                    for q in range(4)
                ]
                u0 = exchange_pair(lane3, 2, v[0], v[2])[h]
                u1 = exchange_pair(lane3, 2, v[1], v[3])[h]
                w0, w1 = exchange_pair(lane3, 1, u0, u1)
                send[h, rx * COLS + 2 * ry] = w0
                send[h, rx * COLS + 2 * ry + 1] = w1

    def forward(h, r, c, source_r, source_c):
        k = r * COLS + c
        return pltpu.make_async_remote_copy(
            src_ref=send.at[h, k],
            dst_ref=place(f0, h, source_r, source_c),
            send_sem=ssem.at[h],
            recv_sem=rsem.at[h],
            device_id=(r, c),
            device_id_type=MESH,
        )

    def send_all(h):
        each_other(lambda r, c: forward(h, r, c, row, col).start())
        f0[h, 4 * row, col] = send[h, me]

    def wait_bytes(ref, sem):
        pltpu.make_async_copy(ref, ref, sem).wait()

    others = pl.ds(0, DEVICES - 1)

    lane2 = lax.broadcasted_iota(jnp.int32, (CLASS_Y, LANES), 1)
    lane = lax.broadcasted_iota(jnp.int32, (1, LANES), 1)
    begin = REST * lax.broadcasted_iota(jnp.int32, (8, 8, LANES), 1)
    lane_8 = lax.broadcasted_iota(jnp.int32, (8, 8, LANES), 2)
    own_lanes = (lane_8 >= begin) & (lane_8 < begin + REST)

    def fill(ref, h, unit):
        for r in range(4):
            for i in range(4):
                here = ref[h, 4 * r, :, i].reshape(CLASS_Y, LANES)
                after = ref[h, 4 * ((r + 1) % 4), :, i].reshape(CLASS_Y, LANES)
                for m in (1, 2, 3):
                    reached = (i < 2 * unit, unit == 4, i >= 4 - 2 * unit)[m - 1]
                    if reached:
                        ref[h, 4 * r + m, :, i] = jnp.where(
                            (lane2 & 3) < 4 - m, roll(here, -m, 1), roll(after, 4 - m, 1)
                        ).reshape(8, 8, LANES)

    def make_taps():
        shape = (2 * LANES, LANES)
        gap = (
            lax.broadcasted_iota(jnp.int32, shape, 0) - lax.broadcasted_iota(jnp.int32, shape, 1)
        ) & (LANES - 1)
        for scale, spacing in enumerate(SPACINGS):
            matrix = jnp.zeros(shape, jnp.float32)
            for k, tap in zip(range(-2, 3), SPLINE_TAPS):
                matrix = jnp.where(gap == (k * spacing) % LANES, tap, matrix)
            taps[scale] = matrix.astype(jnp.bfloat16)

    def smooth_rows(src, dst, h, scale, r, acc):
        unit = SPACINGS[scale] // 4
        mids = []
        for i in range(4):

            def at(k):
                n = i + k * unit
                block = 4 * r + n // 4
                block = jnp.where(block < 0, block + 16, jnp.where(block >= 16, block - 16, block))
                return src[h, block, :, n % 4].reshape(CLASS_Y, LANES)

            mids.append(at(0))
            v = five_taps(at(-2), at(-1), mids[i], at(1), at(2))
            padded[i, 8:72, :] = v
            padded[i, 0:8, :] = v[56:]
            padded[i, 72:80, :] = v[:8]
        rows = []
        for i in range(4):
            rows.append(
                five_taps(*(padded[i, 8 + k * unit : 72 + k * unit, :] for k in range(-2, 3)))
            )
        v = jnp.concatenate(rows, axis=0)
        high = v.astype(jnp.bfloat16)
        low = (v - high.astype(jnp.float32)).astype(jnp.bfloat16)
        v = jnp.dot(
            jnp.concatenate([high, low], axis=1), taps[scale], preferred_element_type=jnp.float32
        )
        for i in range(4):
            smooth = v[CLASS_Y * i : CLASS_Y * (i + 1)]
            if scale < len(SPACINGS) - 1:
                dst[h, 4 * r, :, i] = smooth.reshape(8, 8, LANES)
            detail = (mids[i] - smooth).reshape(8, 8, LANES)
            square = detail * detail
            parts = (jnp.abs(detail), square, square * detail, square * square)
            acc = tuple(s + jnp.sum(p, axis=0) for s, p in zip(acc, parts))
        if scale == len(SPACINGS) - 1:
            last = v[3 * CLASS_Y :]
            for j in range(3):
                row_j = v[CLASS_Y * j : CLASS_Y * (j + 1)]
                t = times(thirds(row_j) + thirds(last), INTO + 768 * j)
                packed[h, pl.ds(8 * r, 8), j] = t.reshape(8, 8, LANES)
            t = times(thirds(last), INTO_REST).reshape(8, 8, LANES)
            t = jnp.sum(jnp.where(own_lanes, t, 0.0), axis=1)
            for c in range(COLS):
                rests[8 * r + c, h] = t[c : c + 1]
        return acc

    def backward(h, r, c, source_r, source_c):
        source = source_r * COLS + source_c
        return pltpu.make_async_remote_copy(
            src_ref=packed.at[h, r * COLS + c],
            dst_ref=back.at[h, source],
            send_sem=bssem.at[h],
            recv_sem=brsem.at[h, source_r],
            device_id=(r, c),
            device_id_type=MESH,
        )

    def scales(h, accs):
        fields = (f0, f1, f0, f1)
        results = []
        for scale, spacing in enumerate(SPACINGS):
            src, dst = fields[scale], fields[scale + 1]
            fill(src, h, spacing // 4)

            acc = accs[scale]
            for near in range(4):
                r = row + near
                r = jnp.where(r >= ROWS, r - ROWS, r)
                acc = smooth_rows(src, dst, h, scale, r, acc)
                if scale == len(SPACINGS) - 1:
                    for hi in planes:
                        for c in (2 * hi + 1 - col_lo, 2 * hi + col_lo):

                            @pl.when(r * COLS + c != me)
                            def _():
                                backward(h, r, c, row, col).start()

            results.append(acc)
        back[h, me] = packed[h, me]
        return results

    make_taps()
    pack(0)
    pl.semaphore_wait(barrier, DEVICES - 1)
    send_all(0)
    pack(1)
    send_all(1)
    accs = [(jnp.zeros((8, LANES), jnp.float32),) * 4] * len(SPACINGS)

    def chunk(h, accs):
        wait_bytes(send.at[h, others], rsem.at[h])
        return scales(h, accs)

    load_basis.wait()
    accs = lax.fori_loop(0, CHUNKS, chunk, accs)

    total = jnp.zeros((1, LANES), jnp.float32)
    for scale, acc in enumerate(accs):
        for moment, s in enumerate(acc):
            value = jnp.sum(jnp.sum(s, axis=0, keepdims=True), axis=1, keepdims=True)
            total = total + jnp.where(lane == 4 * scale + moment, value, 0.0)
    for k in range(DEVICES):
        rests[k, 2] = total
    sums[me] = rests[me]

    def share(r, c, source):
        return pltpu.make_async_remote_copy(
            src_ref=rests.at[r * COLS + c],
            dst_ref=sums.at[source],
            send_sem=mssem,
            recv_sem=mrsem,
            device_id=(r, c),
            device_id_type=MESH,
        )

    each_other(lambda r, c: share(r, c, me).start())

    def wait_back(h, rx):
        @pl.when(rx == row)
        def _():
            wait_bytes(packed.at[h, pl.ds(0, COLS - 1)], brsem.at[h, rx])

        @pl.when(rx != row)
        def _():
            wait_bytes(packed.at[h, pl.ds(0, COLS)], brsem.at[h, rx])

    def back_thirds(h, rx):
        return [thirds(back[h, pl.ds(8 * rx, 8), k].reshape(CLASS_Y, LANES)) for k in range(3)]

    @pl.loop(0, 4)
    def _(j):
        rx = row - j
        rx = jnp.where(rx < 0, rx + ROWS, rx)
        wait_back(0, rx)
        parts = back_thirds(0, rx)
        for k in range(3):
            f0[0, rx, :, k] = times(parts[k], OUT).reshape(8, 8, LANES)
        f0[0, rx, :, 3] = times(sum(parts, []), OUT_LAST).reshape(8, 8, LANES)

    wait_bytes(sums.at[others], mrsem)

    @pl.loop(0, 4)
    def _(j):
        rx = lax.rem(row + 4 - j, 4)
        wait_back(1, rx)
        rows = []
        for h in range(CHUNKS):
            rest = jnp.stack([jnp.broadcast_to(sums[8 * rx + c, h], (8, LANES)) for c in range(COLS)])
            rest = thirds(jnp.where(own_lanes, rest, 0.0).reshape(CLASS_Y, LANES))
            if h == 0:
                lines = [f0[0, rx, :, k].reshape(CLASS_Y, LANES) for k in range(4)]
                lines[3] = lines[3] + times(rest, OUT_LAST + 1152)
            else:
                parts = back_thirds(h, rx)
                lines = [times(t, OUT) for t in parts] + [times(sum(parts, []) + rest, OUT_LAST)]
            rows.append(lines)
        for ry in range(4):
            u = []
            for h in range(CHUNKS):
                w = [
                    jnp.stack([v[8 * c : 8 * c + 8] for v in rows[h]])
                    for c in (2 * ry, 2 * ry + 1)
                ]
                u.append(exchange_pair(lane3, 1, w[0], w[1]))
            for q in range(2):
                for low, v in enumerate(exchange_pair(lane3, 2, u[0][q], u[1][q])):
                    for i in range(4):
                        out_ref[4 * (q + 2 * low) + i, rx, pl.ds(ry, 8, stride=4), :] = v[i]

    wait_bytes(sums.at[others], mssem)
    for h in range(CHUNKS):
        wait_bytes(send.at[h, others], ssem.at[h])
        wait_bytes(packed.at[h, others], bssem.at[h])

    means = sum(sums[k, 2] for k in range(DEVICES)) / jnp.float32(SUB * SUB * LANES)
    moment = lane & 3
    second = jnp.where(moment == 2, roll(means, 1, 1), roll(means, 2, 1)) + EPSILON
    power = second * jnp.where(moment == 2, jnp.sqrt(second), second)
    final = jnp.where(moment < 2, means, means / power)
    for scale in range(len(SPACINGS)):
        tab_ref[scale] = final[:, 4 * scale : 4 * scale + 4]


def per_device_classes(density):
    size_x, size_y, planes = density.shape
    dma = pltpu.SemaphoreType.DMA((CHUNKS,))
    block = pltpu.VMEM((CHUNKS, DEVICES, 4, 8, LANES), jnp.float32)
    part = pltpu.VMEM((CHUNKS, DEVICES, 3, 8, LANES), jnp.float32)
    rests = pltpu.VMEM((DEVICES, 3, 1, LANES), jnp.float32)
    field = pltpu.VMEM((CHUNKS, CLASS_X // 4, CLASS_Y // 8, 4, 8, LANES), jnp.float32)
    coarse, moments = pl.pallas_call(
        class_kernel,
        out_shape=(
            jax.ShapeDtypeStruct((16, 4, size_y, planes), jnp.float32),
            jax.ShapeDtypeStruct((len(SPACINGS), 1, 4), jnp.float32),
        ),
        in_specs=[pl.BlockSpec(memory_space=pltpu.HBM)] * 2,
        out_specs=(pl.BlockSpec(memory_space=pltpu.VMEM),) * 2,
        scratch_shapes=[
            pltpu.VMEM((16, 4, size_y, planes), jnp.float32),
            block,
            field,
            field,
            part,
            pltpu.VMEM((4, CLASS_Y + 16, LANES), jnp.float32),
            pltpu.VMEM((len(SPACINGS), 2 * LANES, LANES), jnp.bfloat16),
            pltpu.VMEM((MATRIX_ROWS, LANES), jnp.bfloat16),
            part,
            rests,
            rests,
        ]
        + [dma] * 3
        + [pltpu.SemaphoreType.DMA((CHUNKS, ROWS))]
        + [pltpu.SemaphoreType.DMA] * 2
        + [pltpu.SemaphoreType.DMA((4,)), pltpu.SemaphoreType.DMA],
        compiler_params=pltpu.CompilerParams(
            collective_id=0, has_side_effects=True, vmem_limit_bytes=32 * 1024 * 1024
        ),
    )(
        pltpu.with_memory_space_constraint(density.reshape(16, 4, size_y, planes), pltpu.HBM),
        pltpu.with_memory_space_constraint(jnp.asarray(range_matrices()), pltpu.HBM),
    )
    return coarse.reshape(size_x, size_y, planes), moments.reshape(len(SPACINGS), 4, 1, 1)


def solution(mesh):
    placed = (P("row", "col", None),)

    def program(density):
        size_x, size_y, planes = density.shape
        local = (size_x // mesh.shape["row"], size_y // mesh.shape["col"], planes)
        classes = (mesh.shape["row"], mesh.shape["col"]) == (ROWS, COLS) and local == BLOCK
        return jax.shard_map(
            per_device_classes if classes else per_device,
            mesh=mesh,
            in_specs=placed,
            out_specs=(P("row", "col", None), P()),
            check_vma=False,
        )(density)

    return program
```
